512 devices in a mesh: gx: 16 (over z_hi, x), gy: 32 (over y, z_lo, core).
Axes of the slice: x: 4, y: 4, z: 16 (z_hi: 4, z_lo: 4; z = z_hi * 4 + z_lo), core: 2. Of those that a mesh axis runs over, the one named last changes fastest.
Arguments:
- features: bfloat16 [16, 32, 1, 8, 8, 8, 128], P('gx', 'gy'), may hold values from -6 to 6
- pre_acts: bfloat16 [2, 16, 32, 1, 8, 8, 8, 128], P(None, 'gx', 'gy'), may hold values from -6 to 6
- cotangent: bfloat16 [16, 32, 1, 8, 8, 8, 128], P('gx', 'gy'), may hold values from -6 to 6
- weights: bfloat16 [2, 27, 128, 128], replicated, may hold values from -0.109375 to 0.109375
- voxel_mask: int32 [16, 32, 1, 512], P('gx', 'gy'), may hold values from 0 to 1, as said below
- neighbours: int32 [16, 32, 1, 27], P('gx', 'gy'), may hold values from -1 to 8, as said below
Outputs:
- grad_input: bfloat16 [16, 32, 1, 8, 8, 8, 128], P('gx', 'gy')
- weight_grads: bfloat16 [2, 27, 128, 128], replicated
The draws below stay inside these ranges and needn't reach their ends.
Inputs may be any that keep to these rules, and one draw needn't show every extreme that they name: `neighbours`: the map is cut into block columns, one a device, each a column of 2 tile positions along the height; the active positions of a block column occupy its first slots in order of height, and the other slots are empty. Entry k of a slot's list names the active tile displaced by (a, b, c) tiles, as (3 (a + 1) + (b + 1)) + its slot on the owning device, or -1 where that position is inactive or off the map; an active tile's entry 13 names itself, all entries of an empty slot are -1, and the lists are symmetric. Every device holds exactly one active tile; both ends of the range are reached. `voxel_mask`: 1 marks an occupied voxel; empty tile slots are all zero.
All inputs are finite; a program needn't handle non-finite values.
Results may differ from the reference program's by a relative error of at most 0.0049.
Values may be sent and summed in bfloat16 or wider, within the bound.
A program may use at most 128 MiB of HBM per device.

```python
import math
import jax
import jax.numpy as jnp

C = 128
LAYERS = 2
TILES = 1
ZSPAN = 2
GRID_X = 16
GRID_Y = 32
VOXELS = 262144


def geometry(key):
    key = jax.random.fold_in(key, 11)
    key_counts, key_row, key_col, key_orders = jax.random.split(key, 4)
    devices_all = GRID_X * GRID_Y
    tile_counts = jax.random.randint(key_counts, (devices_all,), 1, TILES + 1)
    fullest_row = jax.random.randint(key_row, (), 1, GRID_X)
    fullest_col = jax.random.randint(key_col, (), 1, GRID_Y)
    fullest = fullest_row * GRID_Y + fullest_col
    partner = (fullest_row - 1) * GRID_Y + fullest_col - 1
    device_ids = jnp.arange(devices_all)
    tile_counts = jnp.where((device_ids == fullest) | (device_ids == partner), TILES, tile_counts).astype(jnp.int32)
    orders = jax.vmap(lambda one_key: jax.random.permutation(one_key, ZSPAN))(jax.random.split(key_orders, devices_all))
    orders = jnp.where((device_ids == partner)[:, None], orders[fullest][None, :], orders)
    ranking = jnp.argsort(orders, axis=1)
    active = ranking < tile_counts[:, None]
    slot_ids = jnp.cumsum(active.astype(jnp.int32), axis=1) - 1
    return (active.reshape(GRID_X, GRID_Y, ZSPAN), slot_ids.astype(jnp.int32).reshape(GRID_X, GRID_Y, ZSPAN), tile_counts.reshape(GRID_X, GRID_Y))


def draw_neighbours(key, part):
    active, slot_ids, tile_counts = geometry(key)
    slot_range = jnp.arange(TILES, dtype=jnp.int32)
    heights_all = jnp.arange(ZSPAN, dtype=jnp.int32)
    matched = active[:, :, None, :] & (slot_ids[:, :, None, :] == slot_range[None, None, :, None])
    heights = jnp.sum(jnp.where(matched, heights_all[None, None, None, :], 0), axis=-1).astype(jnp.int32)
    filled = slot_range[None, None, :] < tile_counts[:, :, None]
    active_pad = jnp.pad(active, ((1, 1), (1, 1), (1, 1)))
    slot_pad = jnp.pad(slot_ids, ((1, 1), (1, 1), (1, 1)), constant_values=-1)
    listing = []
    for a in (-1, 0, 1):
        for b in (-1, 0, 1):
            for c in (-1, 0, 1):
                shifted_active = active_pad[1 + a:1 + a + GRID_X, 1 + b:1 + b + GRID_Y]
                shifted_slots = slot_pad[1 + a:1 + a + GRID_X, 1 + b:1 + b + GRID_Y]
                target = heights + 1 + c
                present = jnp.take_along_axis(shifted_active, target, axis=2)
                target_slot = jnp.take_along_axis(shifted_slots, target, axis=2)
                owner_code = (a + 1) * 3 + (b + 1)
                listing.append(jnp.where(filled & present, owner_code * TILES + target_slot, -1))
    return jnp.stack(listing, axis=-1).astype(jnp.int32)


def draw_voxel_mask(key, part):
    active, slot_ids, tile_counts = geometry(key)
    key = jax.random.fold_in(key, 5)
    filled = jnp.arange(TILES, dtype=jnp.int32)[None, None, :] < tile_counts[:, :, None]
    coin_flips = jax.random.randint(key, (GRID_X, GRID_Y, TILES, 512), 0, 8) < 5
    return (coin_flips & filled[..., None]).astype(jnp.int32)


def steps_of(own_key, dims, cuts, least, high):
    gain, own = 1.0, jax.random.fold_in(own_key, 6)
    for dim, blocks in cuts:
        draws = jnp.exp(jax.random.uniform(jax.random.fold_in(own, dim), (blocks,), jnp.float32, least / len(cuts), high / len(cuts)))
        gain = gain * jnp.repeat(draws, dims[dim] // blocks).reshape([-1 if axis == dim else 1 for axis in range(len(dims))])
    return gain


def bell_draw(rng, dims, scale, bound, cuts=(), held_as=jnp.bfloat16):
    gain = steps_of(rng, dims, cuts, -0.22, 0.18) if cuts else 1.0
    entries = jax.random.normal(rng, dims, jnp.float32) * scale * gain
    return jnp.minimum(jnp.maximum(entries, -bound), bound).astype(held_as)


def setup_inputs(seed: int = 0) -> dict:
    key_list = jax.random.split(jax.random.key(seed), 7)
    features = bell_draw(key_list[0], (GRID_X, GRID_Y, TILES, 8, 8, 8, C), 1.0, 6.0, ((0, 16), (1, 32)))
    pre_acts = bell_draw(key_list[1], (LAYERS, GRID_X, GRID_Y, TILES, 8, 8, 8, C), 1.0, 6.0, ((1, 16), (2, 32)))
    cotangent = bell_draw(key_list[2], (GRID_X, GRID_Y, TILES, 8, 8, 8, C), 1.0, 6.0, ((0, 16), (1, 32)))
    weights = bell_draw(key_list[3], (LAYERS, 27, C, C), (27 * C) ** -0.5, 0.109375)
    voxel_mask = draw_voxel_mask(jax.random.fold_in(key_list[6], 71), 0)
    neighbours = draw_neighbours(jax.random.fold_in(key_list[6], 71), 0)
    return {"features": features, "pre_acts": pre_acts, "cotangent": cotangent, "weights": weights, "voxel_mask": voxel_mask, "neighbours": neighbours}


def rim_slice(offset):
    if offset < 0:
        return slice(7, 8)
    if offset > 0:
        return slice(0, 1)
    return slice(0, 8)

def assemble(source, lookup):
    planes = []
    for a in (-1, 0, 1):
        y_parts = []
        for b in (-1, 0, 1):
            z_parts = []
            for c in (-1, 0, 1):
                k = (a + 1) * 9 + (b + 1) * 3 + (c + 1)
                rim_part = source[:, rim_slice(a), rim_slice(b), rim_slice(c)]
                z_parts.append(jnp.take(rim_part, lookup[:, k], axis=0))
            y_parts.append(jnp.concatenate(z_parts, axis=3))
        planes.append(jnp.concatenate(y_parts, axis=2))
    return jnp.concatenate(planes, axis=1)

def weight_terms(padded_in, out_grad, channels):
    flat_grad = out_grad.reshape(-1, channels)
    kernel_terms = []
    for a in (-1, 0, 1):
        for b in (-1, 0, 1):
            for c in (-1, 0, 1):
                window = padded_in[:, 1 + a:9 + a, 1 + b:9 + b, 1 + c:9 + c].reshape(-1, channels)
                kernel_terms.append(jnp.dot(window.T, flat_grad, preferred_element_type=jnp.float32))
    return jnp.stack(kernel_terms)

def input_terms(padded_grad, kernels, channels):
    tile_total = padded_grad.shape[0]
    running = jnp.zeros((tile_total * 512, channels), jnp.float32)
    for a in (-1, 0, 1):
        for b in (-1, 0, 1):
            for c in (-1, 0, 1):
                k = (a + 1) * 9 + (b + 1) * 3 + (c + 1)
                window = padded_grad[:, 1 - a:9 - a, 1 - b:9 - b, 1 - c:9 - c].reshape(-1, channels)
                running = running + jnp.dot(window, kernels[k].T, preferred_element_type=jnp.float32)
    return running.reshape(tile_total, 8, 8, 8, channels)

def reference(features, pre_acts, cotangent, weights, voxel_mask, neighbours):
    tile_total = GRID_X * GRID_Y * TILES
    voxel_on = voxel_mask.reshape(tile_total, 8, 8, 8, 1) > 0
    zero_value = jnp.zeros((), jnp.bfloat16)
    zero_tile = jnp.zeros((1, 8, 8, 8, C), jnp.bfloat16)
    listed = neighbours.reshape(tile_total, 27)
    owner_code = jnp.where(listed < 0, 4 * TILES, listed) // TILES
    slot_ids = jnp.where(listed < 0, 0, listed) % TILES
    home_dev = (jnp.arange(tile_total, dtype=jnp.int32) // TILES)[:, None]
    row_dev = home_dev // GRID_Y + owner_code // 3 - 1
    col_dev = home_dev % GRID_Y + owner_code % 3 - 1
    lookup = jnp.where(listed < 0, tile_total, (row_dev * GRID_Y + col_dev) * TILES + slot_ids).astype(jnp.int32)

    def surround(tile_data):
        return assemble(jnp.concatenate([tile_data, zero_tile], axis=0), lookup)
    pre_flat = pre_acts.reshape(LAYERS, tile_total, 8, 8, 8, C)
    first = features.reshape(1, tile_total, 8, 8, 8, C)
    stacked = jnp.concatenate([first, jnp.maximum(pre_flat[:LAYERS - 1], zero_value)], axis=0)
    inputs = jnp.where(voxel_on, stacked, zero_value)
    out_grad = jnp.where(voxel_on & (pre_flat[LAYERS - 1] > 0), cotangent.reshape(tile_total, 8, 8, 8, C), zero_value)
    norm_scale = 1.0 / math.sqrt(VOXELS)
    collected = [None] * LAYERS
    grad_input = None
    for layer_no in reversed(range(LAYERS)):
        kernel_sums = weight_terms(surround(inputs[layer_no]), out_grad, C)
        collected[layer_no] = (kernel_sums * norm_scale).astype(jnp.bfloat16)
        grad_in = input_terms(surround(out_grad), weights[layer_no], C)
        if layer_no > 0:
            out_grad = jnp.where(voxel_on & (pre_flat[layer_no - 1] > 0), grad_in, 0.0).astype(jnp.bfloat16)
        else:
            grad_input = jnp.where(voxel_on, grad_in, 0.0).astype(jnp.bfloat16)
    return (grad_input.reshape(GRID_X, GRID_Y, TILES, 8, 8, 8, C), jnp.stack(collected))
```

```python
import jax
import jax.numpy as jnp
from jax import lax
from jax.experimental import pallas as pl
from jax.experimental.pallas import tpu as pltpu
from jax.sharding import PartitionSpec as P

F32 = jnp.float32
BF16 = jnp.bfloat16
MESH = pl.DeviceIdType.MESH
SIDES = [(a, b) for a in (-1, 0, 1) for b in (-1, 0, 1) if (a, b) != (0, 0)]
CHUNK = 112


def kernel(
    feat, pre, cot, mask, nbr, w_hbm, gin, wg,
    wv, maskv, pad, pg, xt, gface, gcorner, rface, rcorner,
    s, crecv, hsum, psend, precv, zsend, zrecv, zfin, ag,
    wsem, osem, hss, hrs, css, crs, pss, prs, zss, zrs, zas, zar, pas, par, cas, car,
):
    gx, gy = lax.axis_index("gx"), lax.axis_index("gy")
    z_hi, x = gx // 4, gx % 4
    y, z_lo, core = gy // 8, (gy // 2) % 4, gy % 2
    other = 1 - core
    plane_me = x * 4 + y
    z_me = z_hi * 4 + z_lo

    def plane_device(i):
        return {"gx": z_hi * 4 + i // 4, "gy": (i % 4) * 8 + z_lo * 2 + core}

    def z_device(i):
        return {"gx": (i // 4) * 4 + x, "gy": y * 8 + (i % 4) * 2 + core}

    core_device = {"gx": gx, "gy": gy + 1 - 2 * core}

    def side_device(a, b):
        return {"gx": (gx + a + 16) % 16, "gy": (gy + b + 32) % 32}

    barrier = pltpu.get_barrier_semaphore()
    for a, b in SIDES:
        pl.semaphore_signal(barrier, inc=1, device_id=side_device(a, b), device_id_type=MESH)
    pl.semaphore_signal(barrier, inc=1, device_id=core_device, device_id_type=MESH)

    def greet(j, carry):
        pl.semaphore_signal(barrier, inc=1, device_id=plane_device((plane_me + j) % 16), device_id_type=MESH)
        pl.semaphore_signal(barrier, inc=1, device_id=z_device((z_me + j) % 16), device_id_type=MESH)
        return carry

    lax.fori_loop(1, 16, greet, 0)
    w_copies = [pltpu.make_async_copy(w_hbm.at[l], wv.at[l], wsem.at[l]) for l in (1, 0)]
    for copy in w_copies:
        copy.start()

    rows = lax.broadcasted_iota(jnp.int32, (128, 128), 0)
    cols = lax.broadcasted_iota(jnp.int32, (128, 128), 1)
    ones = jnp.ones((128, 128), BF16)
    for r in range(4):
        line = (mask[:, r * 128 : (r + 1) * 128] > 0).astype(F32)
        spread = jnp.where(rows == cols, jnp.broadcast_to(line, (128, 128)), 0.0).astype(BF16)
        maskv[r * 128 : (r + 1) * 128] = jnp.dot(spread, ones, preferred_element_type=F32)

    def flag(a, b, c):
        return jnp.where(nbr[0, (a + 1) * 9 + (b + 1) * 3 + c + 1] >= 0, 1.0, 0.0)

    level = lax.broadcasted_iota(jnp.int32, (1, 8, 128), 1)

    def place(a, b, tile):
        low, mid, high = flag(a, b, -1), flag(a, b, 0), flag(a, b, 1)
        nx, ny = (1 if a else 8), (1 if b else 8)
        x0, y0 = {-1: 0, 0: 1, 1: 9}[a], {-1: 0, 0: 1, 1: 9}[b]
        shape = (nx, ny, 8, 128)
        below = pltpu.roll(tile, 1, 1) * jnp.where(level == 0, low, mid)
        above = pltpu.roll(tile, 7, 1) * jnp.where(level == 7, high, mid)
        pad[0, x0 : x0 + nx, y0 : y0 + ny] = below.reshape(shape)
        pad[1, x0 : x0 + nx, y0 : y0 + ny] = (tile * mid).reshape(shape)
        pad[2, x0 : x0 + nx, y0 : y0 + ny] = above.reshape(shape)

    def side_copies(l):
        copies = []
        for n, (a, b) in enumerate(SIDES):
            m = SIDES.index((-a, -b))
            if a and b:
                i, j = (a + 1) + (b + 1) // 2, (1 - a) + (1 - b) // 2
                src, dst = gcorner.at[l, i], rcorner.at[l, j]
            else:
                i = (a + 1) // 2 if a else 2 + (b + 1) // 2
                j = (1 - a) // 2 if a else 2 + (1 - b) // 2
                src, dst = gface.at[l, i], rface.at[l, j]
            copies.append(
                pltpu.make_async_remote_copy(
                    src_ref=src, dst_ref=dst, send_sem=hss.at[l, n], recv_sem=hrs.at[l, m],
                    device_id=side_device(a, b), device_id_type=MESH,
                )
            )
        return copies

    def stage(l, g):
        g4 = g.reshape(8, 8, 8, 128)
        for i, e in ((0, 0), (1, 7)):
            gface[l, i] = g4[e].reshape(64, 128).astype(BF16)
            gface[l, 2 + i] = g4[:, e].reshape(64, 128).astype(BF16)
            for j, f in ((0, 0), (1, 7)):
                cell = g4[e, f]
                gcorner[l, 2 * i + j] = jnp.concatenate([cell, cell], axis=0).astype(BF16)

    def rims(l):
        for a, b in SIDES:
            if a and b:
                place(a, b, rcorner[l, (a + 1) + (b + 1) // 2].astype(F32)[:8].reshape(1, 8, 128))
            else:
                i = (a + 1) // 2 if a else 2 + (b + 1) // 2
                place(a, b, rface[l, i].astype(F32).reshape(8, 8, 128))

    def patches():
        for k in range(27):
            a, b, c = k // 9 - 1, (k // 3) % 3 - 1, k % 3 - 1
            window = pad[1 - c, 1 - a : 9 - a, 1 - b : 9 - b]
            pg[:, k * 128 : (k + 1) * 128] = window.reshape(512, 128).astype(BF16)

    def input_grads(l):
        kernels = jnp.concatenate([wv[l, k] for k in range(27)], axis=1)
        return lax.dot_general(
            pg[:, : 27 * 128], kernels, (((1,), (1,)), ((), ())), preferred_element_type=F32
        )

    def kernel_grads(l):
        for m in range(14):
            both = jnp.dot(xt[l], pg[:, m * 256 : (m + 1) * 256], preferred_element_type=F32)
            for h in (0, 1):
                half = both[h * 64 : (h + 1) * 64]
                s[l, h, m * 128 : m * 128 + 64] = half[:, :128]
                s[l, h, m * 128 + 64 : (m + 1) * 128] = half[:, 128:]

    def core_copy(l):
        return pltpu.make_async_remote_copy(
            src_ref=s.at[l, other], dst_ref=crecv.at[l], send_sem=css.at[l], recv_sem=crs.at[l],
            device_id=core_device, device_id_type=MESH,
        )

    def plane_copy(l, j):
        peer = (plane_me + j) % 16
        return pltpu.make_async_remote_copy(
            src_ref=psend.at[l, peer], dst_ref=precv.at[l, j - 1],
            send_sem=pss.at[l, j - 1], recv_sem=prs.at[l, j - 1],
            device_id=plane_device(peer), device_id_type=MESH,
        )

    def z_copy(l, j):
        peer = (z_me + j) % 16
        return pltpu.make_async_remote_copy(
            src_ref=zsend.at[l, peer], dst_ref=zrecv.at[l, j - 1],
            send_sem=zss.at[l, j - 1], recv_sem=zrs.at[l, j - 1],
            device_id=z_device(peer), device_id_type=MESH,
        )

    def z_back(l, j):
        return pltpu.make_async_remote_copy(
            src_ref=zfin.at[l, z_me], dst_ref=zfin.at[l, z_me],
            send_sem=zas.at[l, j - 1], recv_sem=zar.at[l, j - 1],
            device_id=z_device((z_me + j) % 16), device_id_type=MESH,
        )

    def plane_back(l, j):
        return pltpu.make_async_remote_copy(
            src_ref=ag.at[l, core, plane_me], dst_ref=ag.at[l, core, plane_me],
            send_sem=pas.at[l, j - 1], recv_sem=par.at[l, j - 1],
            device_id=plane_device((plane_me + j) % 16), device_id_type=MESH,
        )

    def core_back(l, j):
        owner = (plane_me + 16 - j) % 16
        return pltpu.make_async_remote_copy(
            src_ref=ag.at[l, core, owner], dst_ref=ag.at[l, core, owner],
            send_sem=cas.at[l, j], recv_sem=car.at[l, j],
            device_id=core_device, device_id_type=MESH,
        )

    def each(first, last, act):
        def step(j, carry):
            act(j)
            return carry

        lax.fori_loop(first, last, step, 0)

    def sum_halves(l):
        core_copy(l).wait_recv()

        def chunk(j):
            i = (plane_me + j) % 16
            at = pl.ds(pl.multiple_of(i * CHUNK, CHUNK), CHUNK)
            total = s[l, core, at] + crecv[l, at]
            psend[l, i] = total.astype(BF16)
            plane_copy(l, j).start()

        each(1, 16, chunk)
        at = pl.ds(pl.multiple_of(plane_me * CHUNK, CHUNK), CHUNK)
        hsum[l] = s[l, core, at] + crecv[l, at]

    def sum_plane(l):
        def add(j, total):
            plane_copy(l, j).wait_recv()
            return total + precv[l, j - 1].astype(F32)

        total = lax.fori_loop(1, 16, add, hsum[l])
        zsend[l, :14] = total.reshape(14, 8, 128)
        zsend[l, 14:] = jnp.zeros((2, 8, 128), F32)
        each(1, 16, lambda j: z_copy(l, j).start())

    def sum_z(l):
        def add(j, total):
            z_copy(l, j).wait_recv()
            return total + zrecv[l, j - 1]

        total = lax.fori_loop(1, 16, add, zsend[l, z_me])
        zfin[l, z_me] = (total * (1.0 / 512.0)).astype(BF16).astype(F32)
        each(1, 16, lambda j: z_back(l, j).start())

    def spread_plane(l):
        each(1, 16, lambda j: z_back(l, j).wait_recv())
        ag[l, core, plane_me] = zfin[l, :14].reshape(CHUNK, 128).astype(BF16)
        each(1, 16, lambda j: plane_back(l, j).start())
        core_back(l, 0).start()

    def forward(l):
        def pass_on(j):
            plane_back(l, j).wait_recv()
            core_back(l, j).start()

        each(1, 16, pass_on)

    def out_copy(l, h):
        return pltpu.make_async_copy(ag.at[l, h], wg.at[l, h], osem.at[l, h])

    on = maskv[...]
    g1 = jnp.where((on > 0) & (pre[1].astype(F32) > 0), cot[...].astype(F32), 0.0)
    stage(1, g1)
    pl.semaphore_wait(barrier, 8 + 1 + 30)
    for copy in side_copies(1):
        copy.start()
    place(0, 0, g1.reshape(64, 8, 128))
    x1 = jnp.where(on > 0, jnp.maximum(pre[0].astype(F32), 0.0), 0.0)
    xt[1] = x1.T.astype(BF16)
    x0 = jnp.where(on > 0, feat[...].astype(F32), 0.0)
    xt[0] = x0.T.astype(BF16)
    pg[:, 27 * 128 :] = jnp.zeros((512, 128), BF16)
    for copy in w_copies:
        copy.wait()
    for copy in side_copies(1):
        copy.wait_recv()
    rims(1)
    patches()
    d1 = input_grads(1)
    g0 = jnp.where((maskv[...] > 0) & (pre[0].astype(F32) > 0), d1, 0.0).astype(BF16).astype(F32)
    stage(0, g0)
    for copy in side_copies(0):
        copy.start()
    place(0, 0, g0.reshape(64, 8, 128))
    kernel_grads(1)
    core_copy(1).start()
    for copy in side_copies(0):
        copy.wait_recv()
    rims(0)
    patches()
    sum_halves(1)
    kernel_grads(0)
    core_copy(0).start()
    d0 = input_grads(0)
    gin[...] = jnp.where(maskv[...] > 0, d0, 0.0).astype(BF16)
    sum_halves(0)
    sum_plane(1)
    sum_z(1)
    sum_plane(0)
    spread_plane(1)
    sum_z(0)
    forward(1)
    spread_plane(0)
    each(0, 16, lambda j: core_back(1, j).wait_recv())
    for h in (0, 1):
        out_copy(1, h).start()
    forward(0)
    each(0, 16, lambda j: core_back(0, j).wait_recv())
    for h in (0, 1):
        out_copy(0, h).start()

    for l in (1, 0):
        for copy in side_copies(l):
            copy.wait_send()
        core_copy(l).wait_send()
        core_back(l, 0).wait_send()

        def sent(j):
            plane_copy(l, j).wait_send()
            z_copy(l, j).wait_send()
            z_back(l, j).wait_send()
            plane_back(l, j).wait_send()
            core_back(l, j).wait_send()

        each(1, 16, sent)
        for h in (0, 1):
            out_copy(l, h).wait()


def on_device(features, pre_acts, cotangent, weights, voxel_mask, neighbours):
    vmem = pl.BlockSpec(memory_space=pltpu.VMEM)
    anywhere = pl.BlockSpec(memory_space=pl.ANY)
    dma = pltpu.SemaphoreType.DMA
    gin, wg = pl.pallas_call(
        kernel,
        out_shape=(
            jax.ShapeDtypeStruct((512, 128), BF16),
            jax.ShapeDtypeStruct((2, 2, 16, CHUNK, 128), BF16),
        ),
        in_specs=[vmem, vmem, vmem, vmem, pl.BlockSpec(memory_space=pltpu.SMEM), anywhere],
        out_specs=(vmem, anywhere),
        scratch_shapes=[
            pltpu.VMEM((2, 27, 128, 128), BF16),
            pltpu.VMEM((512, 128), F32),
            pltpu.VMEM((3, 10, 10, 8, 128), F32),
            pltpu.VMEM((512, 28 * 128), BF16),
            pltpu.VMEM((2, 128, 512), BF16),
            pltpu.VMEM((2, 4, 64, 128), BF16),
            pltpu.VMEM((2, 4, 16, 128), BF16),
            pltpu.VMEM((2, 4, 64, 128), BF16),
            pltpu.VMEM((2, 4, 16, 128), BF16),
            pltpu.VMEM((2, 2, 16 * CHUNK, 128), F32),
            pltpu.VMEM((2, 16 * CHUNK, 128), F32),
            pltpu.VMEM((2, CHUNK, 128), F32),
            pltpu.VMEM((2, 16, CHUNK, 128), BF16),
            pltpu.VMEM((2, 15, CHUNK, 128), BF16),
            pltpu.VMEM((2, 16, 8, 128), F32),
            pltpu.VMEM((2, 15, 8, 128), F32),
            pltpu.VMEM((2, 16, 8, 128), F32),
            pltpu.VMEM((2, 2, 16, CHUNK, 128), BF16),
            dma((2,)), dma((2, 2)), dma((2, 8)), dma((2, 8)), dma((2,)), dma((2,)),
            dma((2, 15)), dma((2, 15)), dma((2, 15)), dma((2, 15)), dma((2, 15)), dma((2, 15)),
            dma((2, 15)), dma((2, 15)), dma((2, 16)), dma((2, 16)),
        ],
        compiler_params=pltpu.CompilerParams(
            collective_id=0, has_side_effects=True, vmem_limit_bytes=48 * 1024 * 1024
        ),
        cost_estimate=pl.CostEstimate(flops=2_000_000_000, bytes_accessed=5_000_000, transcendentals=0),
    )(
        features.reshape(512, 128),
        pre_acts.reshape(2, 512, 128),
        cotangent.reshape(512, 128),
        voxel_mask.reshape(1, 512),
        neighbours.reshape(1, 27),
        weights,
    )
    halves = wg.reshape(2, 2, 28, 64, 128)[:, :, :27]
    return gin.reshape(1, 1, 1, 8, 8, 8, 128), jnp.swapaxes(halves, 1, 2).reshape(2, 27, 128, 128)


def solution(mesh):
    in_specs = (
        P("gx", "gy", None, None, None, None, None),
        P(None, "gx", "gy", None, None, None, None, None),
        P("gx", "gy", None, None, None, None, None),
        P(),
        P("gx", "gy", None, None),
        P("gx", "gy", None, None),
    )
    out_specs = (P("gx", "gy", None, None, None, None, None), P())
    return jax.shard_map(
        on_device, mesh=mesh, in_specs=in_specs, out_specs=out_specs, check_vma=False
    )
```

```python
import jax
import jax.numpy as jnp
from jax import lax
from jax.experimental import pallas as pl
from jax.experimental.pallas import tpu as pltpu
from jax.sharding import PartitionSpec as P

F32 = jnp.float32
BF16 = jnp.bfloat16
MESH = pl.DeviceIdType.MESH
SIDES = [(a, b) for a in (-1, 0, 1) for b in (-1, 0, 1) if (a, b) != (0, 0)]
CHUNK = 112


def kernel(
    feat_any, pre_any, cot_any, mask_any, nbr_any, w_any, gin, wg,
    feat, pre, cot, mask, nbr, wv, maskv, pad, pg, rowsT, gface, gcorner, rface, rcorner,
    s, crecv, hsum, psend, precv, zsend, zrecv, zfin, ag,
    isem, wsem, osem, hss, hrs, css, crs, pss, prs, zss, zrs, zas, zar, pas, par, cas, car,
):
    gx, gy = lax.axis_index("gx"), lax.axis_index("gy")
    z_hi, x = gx // 4, gx % 4
    y, z_lo, core = gy // 8, (gy // 2) % 4, gy % 2
    other = 1 - core
    plane_me = x * 4 + y
    z_me = z_hi * 4 + z_lo

    def plane_device(i):
        return {"gx": z_hi * 4 + i // 4, "gy": (i % 4) * 8 + z_lo * 2 + core}

    def z_device(i):
        return {"gx": (i // 4) * 4 + x, "gy": y * 8 + (i % 4) * 2 + core}

    core_device = {"gx": gx, "gy": gy + 1 - 2 * core}

    def side_device(a, b):
        return {"gx": (gx + a + 16) % 16, "gy": (gy + b + 32) % 32}

    inputs = [
        pltpu.make_async_copy(src, dst, isem.at[n])
        for n, (src, dst) in enumerate(
            ((mask_any, mask), (nbr_any, nbr), (cot_any, cot), (pre_any, pre), (feat_any, feat))
        )
    ]
    for copy in inputs:
        copy.start()

    barrier = pltpu.get_barrier_semaphore()
    for a, b in SIDES:
        pl.semaphore_signal(barrier, inc=1, device_id=side_device(a, b), device_id_type=MESH)
    pl.semaphore_signal(barrier, inc=1, device_id=core_device, device_id_type=MESH)

    def greet(j, carry):
        pl.semaphore_signal(barrier, inc=1, device_id=plane_device((plane_me + j) % 16), device_id_type=MESH)
        pl.semaphore_signal(barrier, inc=1, device_id=z_device((z_me + j) % 16), device_id_type=MESH)
        return carry

    lax.fori_loop(1, 16, greet, 0)
    w_copies = [pltpu.make_async_copy(w_any.at[l], wv.at[l], wsem.at[l]) for l in (1, 0)]
    for copy in w_copies:
        copy.start()

    for copy in inputs:
        copy.wait()
    rows = lax.broadcasted_iota(jnp.int32, (128, 128), 0)
    cols = lax.broadcasted_iota(jnp.int32, (128, 128), 1)
    ones = jnp.ones((128, 128), BF16)
    for r in range(4):
        line = (mask[:, r * 128 : (r + 1) * 128] > 0).astype(F32)
        spread = jnp.where(rows == cols, jnp.broadcast_to(line, (128, 128)), 0.0).astype(BF16)
        maskv[r * 128 : (r + 1) * 128] = jnp.dot(spread, ones, preferred_element_type=F32)

    def flag(a, b, c):
        return jnp.where(nbr[0, (a + 1) * 9 + (b + 1) * 3 + c + 1] >= 0, 1.0, 0.0)

    level = lax.broadcasted_iota(jnp.int32, (1, 8, 128), 1)

    def place(f, a, b, tile):
        low, mid, high = flag(a, b, -1), flag(a, b, 0), flag(a, b, 1)
        nx, ny = (1 if a else 8), (1 if b else 8)
        x0, y0 = {-1: 0, 0: 1, 1: 9}[a], {-1: 0, 0: 1, 1: 9}[b]
        shape = (nx, ny, 8, 128)
        below = pltpu.roll(tile, 1, 1) * jnp.where(level == 0, low, mid)
        above = pltpu.roll(tile, 7, 1) * jnp.where(level == 7, high, mid)
        pad[f, 0, x0 : x0 + nx, y0 : y0 + ny] = below.reshape(shape)
        pad[f, 1, x0 : x0 + nx, y0 : y0 + ny] = (tile * mid).reshape(shape)
        pad[f, 2, x0 : x0 + nx, y0 : y0 + ny] = above.reshape(shape)

    def side_copies(h):
        copies = []
        for n, (a, b) in enumerate(SIDES):
            m = SIDES.index((-a, -b))
            if a and b:
                i, j = (a + 1) + (b + 1) // 2, (1 - a) + (1 - b) // 2
                src, dst = gcorner.at[h, i], rcorner.at[h, j]
            else:
                i = (a + 1) // 2 if a else 2 + (b + 1) // 2
                j = (1 - a) // 2 if a else 2 + (1 - b) // 2
                src, dst = gface.at[h, i], rface.at[h, j]
            copies.append(
                pltpu.make_async_remote_copy(
                    src_ref=src, dst_ref=dst, send_sem=hss.at[h, n], recv_sem=hrs.at[h, m],
                    device_id=side_device(a, b), device_id_type=MESH,
                )
            )
        return copies

    def stage(h, v):
        v4 = v.reshape(8, 8, 8, 128)
        for i, e in ((0, 0), (1, 7)):
            gface[h, i] = v4[e].reshape(64, 128).astype(BF16)
            gface[h, 2 + i] = v4[:, e].reshape(64, 128).astype(BF16)
            for j, f in ((0, 0), (1, 7)):
                cell = v4[e, f]
                gcorner[h, 2 * i + j] = jnp.concatenate([cell, cell], axis=0).astype(BF16)

    def rims(h, f):
        for copy in side_copies(h):
            copy.wait_recv()
        for a, b in SIDES:
            if a and b:
                cell = rcorner[h, (a + 1) + (b + 1) // 2].astype(F32)[:8]
                place(f, a, b, cell.reshape(1, 8, 128))
            else:
                i = (a + 1) // 2 if a else 2 + (b + 1) // 2
                place(f, a, b, rface[h, i].astype(F32).reshape(8, 8, 128))

    def patches(f, sign):
        for k in range(27):
            a, b, c = (sign * v for v in (k // 9 - 1, (k // 3) % 3 - 1, k % 3 - 1))
            window = pad[f, 1 + c, 1 + a : 9 + a, 1 + b : 9 + b]
            pg[f, :, k * 128 : (k + 1) * 128] = window.reshape(512, 128).astype(BF16)

    def input_grads(l):
        kernels = jnp.concatenate([wv[l, k] for k in range(27)], axis=1)
        return lax.dot_general(
            pg[0, :, : 27 * 128], kernels, (((1,), (1,)), ((), ())), preferred_element_type=F32
        )

    def kernel_grads(l):
        f = 1 - l
        for m in range(14):
            both = jnp.dot(
                rowsT[f], pg[f, :, m * 256 : (m + 1) * 256], preferred_element_type=F32
            )
            for q in (0, 1):
                block = both[:, q * 128 : (q + 1) * 128]
                block = block.T if l == 0 else block
                for h in (0, 1):
                    at = m * 128 + q * 64
                    s[l, h, at : at + 64] = block[h * 64 : (h + 1) * 64]

    def part(i):
        return pl.ds(pl.multiple_of(i * CHUNK, CHUNK), CHUNK)

    def core_copy(l):
        return pltpu.make_async_remote_copy(
            src_ref=s.at[l, other], dst_ref=crecv.at[l], send_sem=css.at[l], recv_sem=crs.at[l],
            device_id=core_device, device_id_type=MESH,
        )

    def plane_copy(l, j):
        peer = (plane_me + j) % 16
        return pltpu.make_async_remote_copy(
            src_ref=psend.at[l, peer], dst_ref=precv.at[l, j - 1],
            send_sem=pss.at[l, j - 1], recv_sem=prs.at[l, j - 1],
            device_id=plane_device(peer), device_id_type=MESH,
        )

    def z_copy(l, j):
        peer = (z_me + j) % 16
        return pltpu.make_async_remote_copy(
            src_ref=zsend.at[l, peer], dst_ref=zrecv.at[l, j - 1],
            send_sem=zss.at[l, j - 1], recv_sem=zrs.at[l, j - 1],
            device_id=z_device(peer), device_id_type=MESH,
        )

    def z_back(l, j):
        return pltpu.make_async_remote_copy(
            src_ref=zfin.at[l, z_me], dst_ref=zfin.at[l, z_me],
            send_sem=zas.at[l, j - 1], recv_sem=zar.at[l, j - 1],
            device_id=z_device((z_me + j) % 16), device_id_type=MESH,
        )

    def plane_back(l, j):
        return pltpu.make_async_remote_copy(
            src_ref=ag.at[l, core, part(plane_me)], dst_ref=ag.at[l, core, part(plane_me)],
            send_sem=pas.at[l, j - 1], recv_sem=par.at[l, j - 1],
            device_id=plane_device((plane_me + j) % 16), device_id_type=MESH,
        )

    def core_back(l, j):
        owner = (plane_me + 16 - j) % 16
        return pltpu.make_async_remote_copy(
            src_ref=ag.at[l, core, part(owner)], dst_ref=ag.at[l, core, part(owner)],
            send_sem=cas.at[l, j], recv_sem=car.at[l, j],
            device_id=core_device, device_id_type=MESH,
        )

    def each(first, last, act):
        def step(j, carry):
            act(j)
            return carry

        lax.fori_loop(first, last, step, 0)

    def sum_halves(l):
        core_copy(l).wait_recv()

        def chunk(j):
            i = (plane_me + j) % 16
            total = s[l, core, part(i)] + crecv[l, part(i)]
            psend[l, i] = total.astype(BF16)
            plane_copy(l, j).start()

        each(1, 16, chunk)
        hsum[l] = s[l, core, part(plane_me)] + crecv[l, part(plane_me)]

    def sum_plane(l):
        def add(j, total):
            plane_copy(l, j).wait_recv()
            return total + precv[l, j - 1].astype(F32)

        total = lax.fori_loop(1, 16, add, hsum[l])
        zsend[l, :14] = total.reshape(14, 8, 128)
        zsend[l, 14:] = jnp.zeros((2, 8, 128), F32)
        each(1, 16, lambda j: z_copy(l, j).start())

    def sum_z(l):
        def add(j, total):
            z_copy(l, j).wait_recv()
            return total + zrecv[l, j - 1]

        total = lax.fori_loop(1, 16, add, zsend[l, z_me])
        zfin[l, z_me] = (total * (1.0 / 512.0)).astype(BF16).astype(F32)
        each(1, 16, lambda j: z_back(l, j).start())

    def spread_plane(l):
        each(1, 16, lambda j: z_back(l, j).wait_recv())
        ag[l, core, part(plane_me)] = zfin[l, :14].reshape(CHUNK, 128).astype(BF16)
        each(1, 16, lambda j: plane_back(l, j).start())
        core_back(l, 0).start()

    def forward(l):
        def pass_on(j):
            plane_back(l, j).wait_recv()
            core_back(l, j).start()

        each(1, 16, pass_on)

    def out_copy(l, h):
        return pltpu.make_async_copy(ag.at[l, h, : 27 * 64], wg.at[l, h], osem.at[l, h])

    on = maskv[...] > 0
    g1 = jnp.where(on & (pre[1].astype(F32) > 0), cot[...].astype(F32), 0.0)
    stage(0, g1)
    x0 = jnp.where(on, feat[...].astype(F32), 0.0)
    stage(1, x0)
    pl.semaphore_wait(barrier, 8 + 1 + 30)
    for h in (0, 1):
        for copy in side_copies(h):
            copy.start()
    place(0, 0, 0, g1.reshape(64, 8, 128))
    place(1, 0, 0, x0.reshape(64, 8, 128))
    x1 = jnp.where(on, jnp.maximum(pre[0].astype(F32), 0.0), 0.0)
    rowsT[0] = x1.T.astype(BF16)
    for f in (0, 1):
        pg[f, :, 27 * 128 :] = jnp.zeros((512, 128), BF16)
    for copy in w_copies:
        copy.wait()

    rims(0, 0)
    patches(0, -1)
    kernel_grads(1)
    core_copy(1).start()
    d1 = input_grads(1)
    g0 = jnp.where((maskv[...] > 0) & (pre[0].astype(F32) > 0), d1, 0.0).astype(BF16).astype(F32)
    stage(2, g0)
    for copy in side_copies(2):
        copy.start()
    rowsT[1] = g0.T.astype(BF16)
    place(0, 0, 0, g0.reshape(64, 8, 128))
    rims(1, 1)
    patches(1, 1)
    sum_halves(1)
    kernel_grads(0)
    core_copy(0).start()
    sum_halves(0)
    rims(2, 0)
    patches(0, -1)
    d0 = input_grads(0)
    gin[...] = jnp.where(maskv[...] > 0, d0, 0.0).astype(BF16)

    sum_plane(1)
    sum_plane(0)
    sum_z(1)
    sum_z(0)
    spread_plane(1)
    spread_plane(0)
    forward(1)
    forward(0)
    for l in (1, 0):
        each(0, 16, lambda j: core_back(l, j).wait_recv())
        for h in (0, 1):
            out_copy(l, h).start()

    for h in (0, 1, 2):
        for copy in side_copies(h):
            copy.wait_send()
    for l in (1, 0):
        core_copy(l).wait_send()
        core_back(l, 0).wait_send()

        def sent(j):
            plane_copy(l, j).wait_send()
            z_copy(l, j).wait_send()
            z_back(l, j).wait_send()
            plane_back(l, j).wait_send()
            core_back(l, j).wait_send()

        each(1, 16, sent)
        for h in (0, 1):
            out_copy(l, h).wait()


def on_device(features, pre_acts, cotangent, weights, voxel_mask, neighbours):
    vmem = pl.BlockSpec(memory_space=pltpu.VMEM)
    anywhere = pl.BlockSpec(memory_space=pl.ANY)
    dma = pltpu.SemaphoreType.DMA
    gin, wg = pl.pallas_call(
        kernel,
        out_shape=(
            jax.ShapeDtypeStruct((512, 128), BF16),
            jax.ShapeDtypeStruct((2, 2, 27 * 64, 128), BF16),
        ),
        in_specs=[anywhere] * 6,
        out_specs=(vmem, anywhere),
        scratch_shapes=[
            pltpu.VMEM((512, 128), BF16),
            pltpu.VMEM((2, 512, 128), BF16),
            pltpu.VMEM((512, 128), BF16),
            pltpu.VMEM((1, 512), jnp.int32),
            pltpu.SMEM((1, 27), jnp.int32),
            pltpu.VMEM((2, 27, 128, 128), BF16),
            pltpu.VMEM((512, 128), F32),
            pltpu.VMEM((2, 3, 10, 10, 8, 128), F32),
            pltpu.VMEM((2, 512, 28 * 128), BF16),
            pltpu.VMEM((2, 128, 512), BF16),
            pltpu.VMEM((3, 4, 64, 128), BF16),
            pltpu.VMEM((3, 4, 16, 128), BF16),
            pltpu.VMEM((3, 4, 64, 128), BF16),
            pltpu.VMEM((3, 4, 16, 128), BF16),
            pltpu.VMEM((2, 2, 16 * CHUNK, 128), F32),
            pltpu.VMEM((2, 16 * CHUNK, 128), F32),
            pltpu.VMEM((2, CHUNK, 128), F32),
            pltpu.VMEM((2, 16, CHUNK, 128), BF16),
            pltpu.VMEM((2, 15, CHUNK, 128), BF16),
            pltpu.VMEM((2, 16, 8, 128), F32),
            pltpu.VMEM((2, 15, 8, 128), F32),
            pltpu.VMEM((2, 16, 8, 128), F32),
            pltpu.VMEM((2, 2, 16 * CHUNK, 128), BF16),
            dma((5,)), dma((2,)), dma((2, 2)), dma((3, 8)), dma((3, 8)), dma((2,)), dma((2,)),
            dma((2, 15)), dma((2, 15)), dma((2, 15)), dma((2, 15)), dma((2, 15)), dma((2, 15)),
            dma((2, 15)), dma((2, 15)), dma((2, 16)), dma((2, 16)),
        ],
        compiler_params=pltpu.CompilerParams(
            collective_id=0, has_side_effects=True, vmem_limit_bytes=64 * 1024 * 1024
        ),
        cost_estimate=pl.CostEstimate(flops=2_000_000_000, bytes_accessed=5_000_000, transcendentals=0),
    )(
        features.reshape(512, 128),
        pre_acts.reshape(2, 512, 128),
        cotangent.reshape(512, 128),
        voxel_mask.reshape(1, 512),
        neighbours.reshape(1, 27),
        weights,
    )
    halves = wg.reshape(2, 2, 27, 64, 128)
    return gin.reshape(1, 1, 1, 8, 8, 8, 128), jnp.swapaxes(halves, 1, 2).reshape(2, 27, 128, 128)


def solution(mesh):
    in_specs = (
        P("gx", "gy", None, None, None, None, None),
        P(None, "gx", "gy", None, None, None, None, None),
        P("gx", "gy", None, None, None, None, None),
        P(),
        P("gx", "gy", None, None),
        P("gx", "gy", None, None),
    )
    out_specs = (P("gx", "gy", None, None, None, None, None), P())
    return jax.shard_map(
        on_device, mesh=mesh, in_specs=in_specs, out_specs=out_specs, check_vma=False
    )
```

```python
import jax
import jax.numpy as jnp
from jax import lax
from jax.experimental import pallas as pl
from jax.experimental.pallas import tpu as pltpu
from jax.sharding import PartitionSpec as P

F32 = jnp.float32
BF16 = jnp.bfloat16
MESH = pl.DeviceIdType.MESH
SIDES = [(a, b) for a in (-1, 0, 1) for b in (-1, 0, 1) if (a, b) != (0, 0)]
BATCHES = ((1, 0, 64, 0), (1, 1024, 48, 8), (0, 0, 64, 0), (0, 1024, 48, 8))
HALF = 27 * 64


def kernel(
    feat_any, pre_any, cot_any, mask_any, nbr_any, w_any, gin, wg,
    feat, pre, cot, mask, nbr, wv, maskv, pad, pg, rowsT, gface, gcorner, rface, rcorner,
    s, crecv, psend, precv, zsend, zrecv, zfin, ag,
    isem, wsem, osem, hss, hrs, css, crs, pss, prs, zss, zrs, zas, zar, pas, par, cas, car,
):
    gx, gy = lax.axis_index("gx"), lax.axis_index("gy")
    z_hi, x = gx // 4, gx % 4
    y, z_lo, core = gy // 8, (gy // 2) % 4, gy % 2
    other = 1 - core
    plane_me = x * 4 + y
    z_me = z_hi * 4 + z_lo

    def plane_device(i):
        return {"gx": z_hi * 4 + i // 4, "gy": (i % 4) * 8 + z_lo * 2 + core}

    def z_device(i):
        return {"gx": (i // 4) * 4 + x, "gy": y * 8 + (i % 4) * 2 + core}

    core_device = {"gx": gx, "gy": gy + 1 - 2 * core}

    def side_device(a, b):
        return {"gx": (gx + a + 16) % 16, "gy": (gy + b + 32) % 32}

    def plane_shift(i):
        v = i + i // 10
        return (2 + v // 4) % 4, (2 + v % 4) % 4

    def plane_to(i):
        dx, dy = plane_shift(i)
        return ((x + dx) % 4) * 4 + (y + dy) % 4

    def plane_from(i):
        dx, dy = plane_shift(i)
        return ((x + 4 - dx) % 4) * 4 + (y + 4 - dy) % 4

    def z_far(i):
        return 8 + (i // 2) - (i % 2) * (2 * (i // 2) + 1)

    inputs = [
        pltpu.make_async_copy(src, dst, isem.at[n])
        for n, (src, dst) in enumerate(
            ((mask_any, mask), (nbr_any, nbr), (cot_any, cot), (pre_any, pre), (feat_any, feat))
        )
    ]
    for copy in inputs:
        copy.start()

    barrier = pltpu.get_barrier_semaphore()
    for a, b in SIDES:
        pl.semaphore_signal(barrier, inc=1, device_id=side_device(a, b), device_id_type=MESH)
    pl.semaphore_signal(barrier, inc=1, device_id=core_device, device_id_type=MESH)

    def greet(j, carry):
        pl.semaphore_signal(barrier, inc=1, device_id=plane_device((plane_me + j) % 16), device_id_type=MESH)
        pl.semaphore_signal(barrier, inc=1, device_id=z_device((z_me + j) % 16), device_id_type=MESH)
        return carry

    lax.fori_loop(1, 16, greet, 0)
    w_copies = [pltpu.make_async_copy(w_any.at[l], wv.at[l], wsem.at[l]) for l in (1, 0)]
    for copy in w_copies:
        copy.start()

    for copy in inputs:
        copy.wait()
    rows = lax.broadcasted_iota(jnp.int32, (128, 128), 0)
    cols = lax.broadcasted_iota(jnp.int32, (128, 128), 1)
    ones = jnp.ones((128, 128), BF16)
    for r in range(4):
        line = (mask[:, r * 128 : (r + 1) * 128] > 0).astype(F32)
        spread = jnp.where(rows == cols, jnp.broadcast_to(line, (128, 128)), 0.0).astype(BF16)
        maskv[r * 128 : (r + 1) * 128] = jnp.dot(spread, ones, preferred_element_type=F32)

    def flag(a, b, c):
        return jnp.where(nbr[0, (a + 1) * 9 + (b + 1) * 3 + c + 1] >= 0, 1.0, 0.0)

    level = lax.broadcasted_iota(jnp.int32, (1, 8, 128), 1)

    def place(f, a, b, tile):
        low, mid, high = flag(a, b, -1), flag(a, b, 0), flag(a, b, 1)
        nx, ny = (1 if a else 8), (1 if b else 8)
        x0, y0 = {-1: 0, 0: 1, 1: 9}[a], {-1: 0, 0: 1, 1: 9}[b]
        shape = (nx, ny, 8, 128)
        below = pltpu.roll(tile, 1, 1) * jnp.where(level == 0, low, mid)
        above = pltpu.roll(tile, 7, 1) * jnp.where(level == 7, high, mid)
        pad[f, 0, x0 : x0 + nx, y0 : y0 + ny] = below.reshape(shape)
        pad[f, 1, x0 : x0 + nx, y0 : y0 + ny] = (tile * mid).reshape(shape)
        pad[f, 2, x0 : x0 + nx, y0 : y0 + ny] = above.reshape(shape)

    def side_copies(group):
        copies = []
        for a, b in SIDES:
            if (group in (0, 3)) != bool(a and b):
                continue
            if a and b:
                i, j = (a + 1) + (b + 1) // 2, (1 - a) + (1 - b) // 2
                src, dst = gcorner.at[group // 3, i], rcorner.at[group // 3, j]
            else:
                i = (a + 1) // 2 if a else 2 + (b + 1) // 2
                j = (1 - a) // 2 if a else 2 + (1 - b) // 2
                face = {1: 0, 2: 1, 4: 2}[group]
                src, dst = gface.at[face, i], rface.at[face, j]
            copies.append(
                pltpu.make_async_remote_copy(
                    src_ref=src, dst_ref=dst, send_sem=hss.at[group, i], recv_sem=hrs.at[group, j],
                    device_id=side_device(a, b), device_id_type=MESH,
                )
            )
        return copies

    def stage_corners(n, first, second):
        for i in (0, 1):
            for j in (0, 1):
                cells = [v.reshape(8, 8, 8, 128)[7 * i, 7 * j] for v in (first, second)]
                gcorner[n, 2 * i + j] = jnp.concatenate(cells, axis=0).astype(BF16)

    def stage_faces(n, v):
        v4 = v.reshape(8, 8, 8, 128)
        for i in (0, 1):
            gface[n, i] = v4[7 * i].reshape(64, 128).astype(BF16)
            gface[n, 2 + i] = v4[:, 7 * i].reshape(64, 128).astype(BF16)

    def rims(f, corners, row, face):
        for a, b in SIDES:
            if a and b:
                cell = rcorner[corners, (a + 1) + (b + 1) // 2].astype(F32)[row : row + 8]
                place(f, a, b, cell.reshape(1, 8, 128))
            else:
                i = (a + 1) // 2 if a else 2 + (b + 1) // 2
                place(f, a, b, rface[face, i].astype(F32).reshape(8, 8, 128))

    def patches(f, sign):
        for k in range(27):
            a, b, c = (sign * v for v in (k // 9 - 1, (k // 3) % 3 - 1, k % 3 - 1))
            window = pad[f, 1 + c, 1 + a : 9 + a, 1 + b : 9 + b]
            pg[f, :, k * 128 : (k + 1) * 128] = window.reshape(512, 128).astype(BF16)

    def input_grads(l):
        kernels = jnp.concatenate([wv[l, k] for k in range(27)], axis=1)
        return lax.dot_general(
            pg[0, :, : 27 * 128], kernels, (((1,), (1,)), ((), ())), preferred_element_type=F32
        )

    def kernel_grads(l, first, last):
        f = 1 - l
        for m in range(first, last):
            both = jnp.dot(
                rowsT[f], pg[f, :, m * 256 : (m + 1) * 256], preferred_element_type=F32
            )
            for q in (0, 1):
                block = both[:, q * 128 : (q + 1) * 128]
                block = block.T if l == 0 else block
                for h in (0, 1):
                    at = m * 128 + q * 64
                    s[l, h, at : at + 64] = block[h * 64 : (h + 1) * 64]

    def part(b, i):
        _, base, chunk, _ = BATCHES[b]
        return pl.ds(pl.multiple_of(base + i * chunk, 16), chunk)

    def core_copy(b):
        l, base, chunk, _ = BATCHES[b]
        rows = pl.ds(base, 16 * chunk)
        return pltpu.make_async_remote_copy(
            src_ref=s.at[l, other, rows], dst_ref=crecv.at[l, rows],
            send_sem=css.at[b], recv_sem=crs.at[b],
            device_id=core_device, device_id_type=MESH,
        )

    def plane_copy(b, i):
        l, _, chunk, _ = BATCHES[b]
        peer = plane_to(i)
        return pltpu.make_async_remote_copy(
            src_ref=psend.at[l, part(b, peer)], dst_ref=precv.at[b, i, pl.ds(0, chunk)],
            send_sem=pss.at[b, i], recv_sem=prs.at[b, i],
            device_id=plane_device(peer), device_id_type=MESH,
        )

    def z_copy(b, o, sender):
        return pltpu.make_async_remote_copy(
            src_ref=zsend.at[b, o], dst_ref=zrecv.at[b, sender],
            send_sem=zss.at[b, o], recv_sem=zrs.at[b, sender],
            device_id=z_device(BATCHES[b][3] + o), device_id_type=MESH,
        )

    def z_back(b, i, o):
        return pltpu.make_async_remote_copy(
            src_ref=zfin.at[b, o], dst_ref=zfin.at[b, o],
            send_sem=zas.at[b, i], recv_sem=zar.at[b, o],
            device_id=z_device((z_me + z_far(i)) % 16), device_id_type=MESH,
        )

    def plane_back(b, i):
        l = BATCHES[b][0]
        rows = part(b, plane_me)
        return pltpu.make_async_remote_copy(
            src_ref=ag.at[l, core, rows], dst_ref=ag.at[l, core, rows],
            send_sem=pas.at[b, i], recv_sem=par.at[b, i],
            device_id=plane_device(plane_to(i)), device_id_type=MESH,
        )

    def core_back(b, n, owner):
        l = BATCHES[b][0]
        rows = part(b, owner)
        return pltpu.make_async_remote_copy(
            src_ref=ag.at[l, core, rows], dst_ref=ag.at[l, core, rows],
            send_sem=cas.at[b, n], recv_sem=car.at[b, n],
            device_id=core_device, device_id_type=MESH,
        )

    def each(first, last, act):
        def step(j, carry):
            act(j)
            return carry

        lax.fori_loop(first, last, step, 0)

    def sum_halves(b):
        l = BATCHES[b][0]
        core_copy(b).wait_recv()

        def chunk(i):
            rows = part(b, plane_to(i))
            psend[l, rows] = (s[l, core, rows] + crecv[l, rows]).astype(BF16)
            plane_copy(b, i).start()

        each(0, 15, chunk)

    def owned(b):
        return z_me - BATCHES[b][3]

    def owns(b):
        return (owned(b) >= 0) & (owned(b) < BATCHES[b][2] // 8)

    def sum_plane(b):
        l, _, chunk, _ = BATCHES[b]

        def add(t, total):
            i = 14 - t
            plane_copy(b, i).wait_recv()
            return total + precv[b, i, pl.ds(0, chunk)].astype(F32)

        rows = part(b, plane_me)
        total = lax.fori_loop(0, 15, add, s[l, core, rows] + crecv[l, rows])
        zsend[b, : chunk // 8] = total.reshape(chunk // 8, 8, 128)

        def send(o):
            @pl.when(owned(b) != o)
            def _():
                z_copy(b, o, z_me).start()

        each(0, chunk // 8, send)

    def sum_z(b):
        @pl.when(owns(b))
        def _():
            o = owned(b)

            def add(t, total):
                sender = (z_me + z_far(14 - t)) % 16
                z_copy(b, o, sender).wait_recv()
                return total + zrecv[b, sender]

            total = lax.fori_loop(0, 15, add, zsend[b, o])
            zfin[b, o] = (total * (1.0 / 512.0)).astype(BF16).astype(F32)
            each(0, 15, lambda i: z_back(b, i, o).start())

    def spread_plane(b):
        l, _, chunk, _ = BATCHES[b]

        def arrive(o):
            @pl.when(owned(b) != o)
            def _():
                z_back(b, 0, o).wait_recv()

        each(0, chunk // 8, arrive)
        ag[l, core, part(b, plane_me)] = zfin[b, : chunk // 8].reshape(chunk, 128).astype(BF16)
        each(0, 15, lambda i: plane_back(b, i).start())
        core_back(b, 15, plane_me).start()

    def out_copy(b, h, n):
        l, base, chunk, _ = BATCHES[b]
        rows = pl.ds(base, min(16 * chunk, HALF - base))
        return pltpu.make_async_copy(ag.at[l, h, rows], wg.at[l, h, rows], osem.at[b, n])

    def forward(b):
        def pass_on(t):
            i = 14 - t
            plane_back(b, i).wait_recv()
            core_back(b, i, plane_from(i)).start()

        each(0, 15, pass_on)
        out_copy(b, core, 0).start()

    def finish(b):
        each(0, 16, lambda n: core_back(b, n, plane_me).wait_recv())
        out_copy(b, other, 1).start()

    on = maskv[...] > 0
    g1 = jnp.where(on & (pre[1].astype(F32) > 0), cot[...].astype(F32), 0.0)
    x0 = jnp.where(on, feat[...].astype(F32), 0.0)
    stage_corners(0, g1, x0)
    stage_faces(0, g1)
    pl.semaphore_wait(barrier, 8 + 1 + 30)
    for group in (0, 1):
        for copy in side_copies(group):
            copy.start()
    stage_faces(1, x0)
    for copy in side_copies(2):
        copy.start()
    place(0, 0, 0, g1.reshape(64, 8, 128))
    place(1, 0, 0, x0.reshape(64, 8, 128))
    x1 = jnp.where(on, jnp.maximum(pre[0].astype(F32), 0.0), 0.0)
    rowsT[0] = x1.T.astype(BF16)
    for f in (0, 1):
        pg[f, :, 27 * 128 :] = jnp.zeros((512, 128), BF16)

    for group in (0, 1):
        for copy in side_copies(group):
            copy.wait_recv()
    rims(0, 0, 0, 0)
    patches(0, -1)
    kernel_grads(1, 0, 8)
    core_copy(0).start()
    kernel_grads(1, 8, 14)
    core_copy(1).start()
    for copy in w_copies:
        copy.wait()
    d1 = input_grads(1)
    g0 = jnp.where((maskv[...] > 0) & (pre[0].astype(F32) > 0), d1, 0.0).astype(BF16).astype(F32)
    stage_corners(1, g0, g0)
    stage_faces(2, g0)
    for group in (3, 4):
        for copy in side_copies(group):
            copy.start()
    rowsT[1] = g0.T.astype(BF16)
    place(0, 0, 0, g0.reshape(64, 8, 128))
    sum_halves(0)
    sum_halves(1)
    for copy in side_copies(2):
        copy.wait_recv()
    rims(1, 0, 8, 1)
    patches(1, 1)
    kernel_grads(0, 0, 8)
    core_copy(2).start()
    kernel_grads(0, 8, 14)
    core_copy(3).start()
    sum_halves(2)
    sum_halves(3)
    sum_plane(0)
    sum_plane(1)
    for group in (3, 4):
        for copy in side_copies(group):
            copy.wait_recv()
    rims(0, 1, 0, 2)
    patches(0, -1)
    d0 = input_grads(0)
    gin[...] = jnp.where(maskv[...] > 0, d0, 0.0).astype(BF16)

    sum_plane(2)
    sum_plane(3)
    for act in (sum_z, spread_plane, forward, finish):
        for b in range(4):
            act(b)

    for group in range(5):
        for copy in side_copies(group):
            copy.wait_send()
    for b in range(4):
        core_copy(b).wait_send()
        core_back(b, 15, plane_me).wait_send()

        def sent(i):
            plane_copy(b, i).wait_send()
            plane_back(b, i).wait_send()
            core_back(b, i, plane_me).wait_send()

        each(0, 15, sent)

        def sent_z(o):
            @pl.when(owned(b) != o)
            def _():
                z_copy(b, o, z_me).wait_send()

        each(0, BATCHES[b][2] // 8, sent_z)

        @pl.when(owns(b))
        def _():
            each(0, 15, lambda i: z_back(b, i, owned(b)).wait_send())

        out_copy(b, core, 0).wait()
        out_copy(b, other, 1).wait()


def on_device(features, pre_acts, cotangent, weights, voxel_mask, neighbours):
    vmem = pl.BlockSpec(memory_space=pltpu.VMEM)
    anywhere = pl.BlockSpec(memory_space=pl.ANY)
    dma = pltpu.SemaphoreType.DMA
    gin, wg = pl.pallas_call(
        kernel,
        out_shape=(
            jax.ShapeDtypeStruct((512, 128), BF16),
            jax.ShapeDtypeStruct((2, 2, HALF, 128), BF16),
        ),
        in_specs=[anywhere] * 6,
        out_specs=(vmem, anywhere),
        scratch_shapes=[
            pltpu.VMEM((512, 128), BF16),
            pltpu.VMEM((2, 512, 128), BF16),
            pltpu.VMEM((512, 128), BF16),
            pltpu.VMEM((1, 512), jnp.int32),
            pltpu.SMEM((1, 27), jnp.int32),
            pltpu.VMEM((2, 27, 128, 128), BF16),
            pltpu.VMEM((512, 128), F32),
            pltpu.VMEM((2, 3, 10, 10, 8, 128), F32),
            pltpu.VMEM((2, 512, 28 * 128), BF16),
            pltpu.VMEM((2, 128, 512), BF16),
            pltpu.VMEM((3, 4, 64, 128), BF16),
            pltpu.VMEM((2, 4, 16, 128), BF16),
            pltpu.VMEM((3, 4, 64, 128), BF16),
            pltpu.VMEM((2, 4, 16, 128), BF16),
            pltpu.VMEM((2, 2, 28 * 64, 128), F32),
            pltpu.VMEM((2, 28 * 64, 128), F32),
            pltpu.VMEM((2, 28 * 64, 128), BF16),
            pltpu.VMEM((4, 15, 64, 128), BF16),
            pltpu.VMEM((4, 8, 8, 128), F32),
            pltpu.VMEM((4, 16, 8, 128), F32),
            pltpu.VMEM((4, 8, 8, 128), F32),
            pltpu.VMEM((2, 2, 28 * 64, 128), BF16),
            dma((5,)), dma((2,)), dma((4, 2)), dma((5, 4)), dma((5, 4)), dma((4,)), dma((4,)),
            dma((4, 15)), dma((4, 15)), dma((4, 8)), dma((4, 16)), dma((4, 15)), dma((4, 8)),
            dma((4, 15)), dma((4, 15)), dma((4, 16)), dma((4, 16)),
        ],
        compiler_params=pltpu.CompilerParams(
            collective_id=0, has_side_effects=True, vmem_limit_bytes=64 * 1024 * 1024
        ),
        cost_estimate=pl.CostEstimate(flops=2_000_000_000, bytes_accessed=5_000_000, transcendentals=0),
    )(
        features.reshape(512, 128),
        pre_acts.reshape(2, 512, 128),
        cotangent.reshape(512, 128),
        voxel_mask.reshape(1, 512),
        neighbours.reshape(1, 27),
        weights,
    )
    halves = wg.reshape(2, 2, 27, 64, 128)
    return gin.reshape(1, 1, 1, 8, 8, 8, 128), jnp.swapaxes(halves, 1, 2).reshape(2, 27, 128, 128)


def solution(mesh):
    in_specs = (
        P("gx", "gy", None, None, None, None, None),
        P(None, "gx", "gy", None, None, None, None, None),
        P("gx", "gy", None, None, None, None, None),
        P(),
        P("gx", "gy", None, None),
        P("gx", "gy", None, None),
    )
    out_specs = (P("gx", "gy", None, None, None, None, None), P())
    return jax.shard_map(
        on_device, mesh=mesh, in_specs=in_specs, out_specs=out_specs, check_vma=False
    )
```

```python
import jax
import jax.numpy as jnp
from jax import lax
from jax.experimental import pallas as pl
from jax.experimental.pallas import tpu as pltpu
from jax.sharding import PartitionSpec as P

F32 = jnp.float32
BF16 = jnp.bfloat16
MESH = pl.DeviceIdType.MESH
SIDES = [(a, b) for a in (-1, 0, 1) for b in (-1, 0, 1) if (a, b) != (0, 0)]
BATCHES = ((1, 0, 64, 0), (1, 1024, 48, 8), (0, 0, 64, 0), (0, 1024, 48, 8))
HALF = 27 * 64


def kernel(
    feat_any, pre_any, cot_any, mask_any, nbr_any, w_any, gin, wg,
    feat, pre, cot, mask, nbr, wv, maskv, pad, pg, rowsT, gface, gcorner, rface, rcorner,
    s, crecv, psend, precv, zsend, zrecv, zfin, ag,
    isem, wsem, osem, hss, hrs, css, crs, pss, prs, zss, zrs, zas, zar, pas, par, cas, car, relays,
):
    gx, gy = lax.axis_index("gx"), lax.axis_index("gy")
    z_hi, x = gx // 4, gx % 4
    y, z_lo, core = gy // 8, (gy // 2) % 4, gy % 2
    other = 1 - core
    plane_me = x * 4 + y
    z_me = z_hi * 4 + z_lo

    def plane_device(i):
        return {"gx": z_hi * 4 + i // 4, "gy": (i % 4) * 8 + z_lo * 2 + core}

    def z_device(i):
        return {"gx": (i // 4) * 4 + x, "gy": y * 8 + (i % 4) * 2 + core}

    core_device = {"gx": gx, "gy": gy + 1 - 2 * core}

    def side_device(a, b):
        return {"gx": (gx + a + 16) % 16, "gy": (gy + b + 32) % 32}

    def plane_shift(i):
        v = i + i // 10
        return (2 + v // 4) % 4, (2 + v % 4) % 4

    def plane_to(i):
        dx, dy = plane_shift(i)
        return ((x + dx) % 4) * 4 + (y + dy) % 4

    def plane_from(i):
        dx, dy = plane_shift(i)
        return ((x + 4 - dx) % 4) * 4 + (y + 4 - dy) % 4

    def z_far(i):
        return 8 + (i // 2) - (i % 2) * (2 * (i // 2) + 1)

    inputs = [
        pltpu.make_async_copy(src, dst, isem.at[n])
        for n, (src, dst) in enumerate(
            ((mask_any, mask), (nbr_any, nbr), (cot_any, cot), (pre_any, pre), (feat_any, feat))
        )
    ]
    for copy in inputs:
        copy.start()

    barrier = pltpu.get_barrier_semaphore()

    def greet(sem, device):
        pl.semaphore_signal(sem, inc=1, device_id=device, device_id_type=MESH)

    def relay(step):
        for shift in (2**step, 16 - 2**step):
            greet(relays.at[step], z_device((z_me + shift) % 16))

    def relayed(step):
        pl.semaphore_wait(relays.at[step], 2)

    for a, b in SIDES:
        greet(barrier, side_device(a, b))
    greet(barrier, core_device)
    for shift in (1, 15):
        greet(barrier, z_device((z_me + shift) % 16))

    def greet_plane(i, carry):
        greet(barrier, plane_device(plane_to(i)))
        return carry

    lax.fori_loop(0, 15, greet_plane, 0)
    w_copies = [pltpu.make_async_copy(w_any.at[l], wv.at[l], wsem.at[l]) for l in (1, 0)]
    for copy in w_copies:
        copy.start()

    for copy in inputs:
        copy.wait()
    rows = lax.broadcasted_iota(jnp.int32, (128, 128), 0)
    cols = lax.broadcasted_iota(jnp.int32, (128, 128), 1)
    ones = jnp.ones((128, 128), BF16)
    for r in range(4):
        line = (mask[:, r * 128 : (r + 1) * 128] > 0).astype(F32)
        spread = jnp.where(rows == cols, jnp.broadcast_to(line, (128, 128)), 0.0).astype(BF16)
        maskv[r * 128 : (r + 1) * 128] = jnp.dot(spread, ones, preferred_element_type=F32)

    def flag(a, b, c):
        return jnp.where(nbr[0, (a + 1) * 9 + (b + 1) * 3 + c + 1] >= 0, 1.0, 0.0)

    level = lax.broadcasted_iota(jnp.int32, (1, 8, 128), 1)

    def place(f, a, b, tile):
        low, mid, high = flag(a, b, -1), flag(a, b, 0), flag(a, b, 1)
        nx, ny = (1 if a else 8), (1 if b else 8)
        x0, y0 = {-1: 0, 0: 1, 1: 9}[a], {-1: 0, 0: 1, 1: 9}[b]
        shape = (nx, ny, 8, 128)
        below = pltpu.roll(tile, 1, 1) * jnp.where(level == 0, low, mid)
        above = pltpu.roll(tile, 7, 1) * jnp.where(level == 7, high, mid)
        pad[f, 0, x0 : x0 + nx, y0 : y0 + ny] = below.reshape(shape)
        pad[f, 1, x0 : x0 + nx, y0 : y0 + ny] = (tile * mid).reshape(shape)
        pad[f, 2, x0 : x0 + nx, y0 : y0 + ny] = above.reshape(shape)

    def side_copies(group):
        copies = []
        for a, b in SIDES:
            if (group in (0, 3)) != bool(a and b):
                continue
            if a and b:
                i, j = (a + 1) + (b + 1) // 2, (1 - a) + (1 - b) // 2
                src, dst = gcorner.at[group // 3, i], rcorner.at[group // 3, j]
            else:
                i = (a + 1) // 2 if a else 2 + (b + 1) // 2
                j = (1 - a) // 2 if a else 2 + (1 - b) // 2
                face = {1: 0, 2: 1, 4: 2}[group]
                src, dst = gface.at[face, i], rface.at[face, j]
            copies.append(
                pltpu.make_async_remote_copy(
                    src_ref=src, dst_ref=dst, send_sem=hss.at[group, i], recv_sem=hrs.at[group, j],
                    device_id=side_device(a, b), device_id_type=MESH,
                )
            )
        return copies

    def stage_corners(n, first, second):
        for i in (0, 1):
            for j in (0, 1):
                cells = [v.reshape(8, 8, 8, 128)[7 * i, 7 * j] for v in (first, second)]
                gcorner[n, 2 * i + j] = jnp.concatenate(cells, axis=0).astype(BF16)

    def stage_faces(n, v):
        v4 = v.reshape(8, 8, 8, 128)
        for i in (0, 1):
            gface[n, i] = v4[7 * i].reshape(64, 128).astype(BF16)
            gface[n, 2 + i] = v4[:, 7 * i].reshape(64, 128).astype(BF16)

    def rims(f, corners, row, face):
        for a, b in SIDES:
            if a and b:
                cell = rcorner[corners, (a + 1) + (b + 1) // 2].astype(F32)[row : row + 8]
                place(f, a, b, cell.reshape(1, 8, 128))
            else:
                i = (a + 1) // 2 if a else 2 + (b + 1) // 2
                place(f, a, b, rface[face, i].astype(F32).reshape(8, 8, 128))

    def patches(f, sign):
        for k in range(27):
            a, b, c = (sign * v for v in (k // 9 - 1, (k // 3) % 3 - 1, k % 3 - 1))
            window = pad[f, 1 + c, 1 + a : 9 + a, 1 + b : 9 + b]
            pg[f, :, k * 128 : (k + 1) * 128] = window.reshape(512, 128).astype(BF16)

    def input_grads(l):
        kernels = jnp.concatenate([wv[l, k] for k in range(27)], axis=1)
        return lax.dot_general(
            pg[0, :, : 27 * 128], kernels, (((1,), (1,)), ((), ())), preferred_element_type=F32
        )

    def kernel_grads(l, first, last):
        f = 1 - l
        for m in range(first, last):
            both = jnp.dot(
                rowsT[f], pg[f, :, m * 256 : (m + 1) * 256], preferred_element_type=F32
            )
            for q in (0, 1):
                block = both[:, q * 128 : (q + 1) * 128]
                block = block.T if l == 0 else block
                for h in (0, 1):
                    at = m * 128 + q * 64
                    s[l, h, at : at + 64] = block[h * 64 : (h + 1) * 64]

    def part(b, i):
        _, base, chunk, _ = BATCHES[b]
        return pl.ds(pl.multiple_of(base + i * chunk, 16), chunk)

    def core_copy(b):
        l, base, chunk, _ = BATCHES[b]
        rows = pl.ds(base, 16 * chunk)
        return pltpu.make_async_remote_copy(
            src_ref=s.at[l, other, rows], dst_ref=crecv.at[l, rows],
            send_sem=css.at[b], recv_sem=crs.at[b],
            device_id=core_device, device_id_type=MESH,
        )

    def plane_copy(b, i):
        l, _, chunk, _ = BATCHES[b]
        peer = plane_to(i)
        return pltpu.make_async_remote_copy(
            src_ref=psend.at[l, part(b, peer)], dst_ref=precv.at[b, i, pl.ds(0, chunk)],
            send_sem=pss.at[b, i], recv_sem=prs.at[b, i],
            device_id=plane_device(peer), device_id_type=MESH,
        )

    def z_copy(b, o, sender):
        return pltpu.make_async_remote_copy(
            src_ref=zsend.at[b, o], dst_ref=zrecv.at[b, sender],
            send_sem=zss.at[b, o], recv_sem=zrs.at[b, sender],
            device_id=z_device(BATCHES[b][3] + o), device_id_type=MESH,
        )

    def z_back(b, i, o):
        return pltpu.make_async_remote_copy(
            src_ref=zfin.at[b, o], dst_ref=zfin.at[b, o],
            send_sem=zas.at[b, i], recv_sem=zar.at[b, o],
            device_id=z_device((z_me + z_far(i)) % 16), device_id_type=MESH,
        )

    def plane_back(b, i):
        l = BATCHES[b][0]
        rows = part(b, plane_me)
        return pltpu.make_async_remote_copy(
            src_ref=ag.at[l, core, rows], dst_ref=ag.at[l, core, rows],
            send_sem=pas.at[b, i], recv_sem=par.at[b, i],
            device_id=plane_device(plane_to(i)), device_id_type=MESH,
        )

    def core_back(b, n, owner):
        l = BATCHES[b][0]
        rows = part(b, owner)
        return pltpu.make_async_remote_copy(
            src_ref=ag.at[l, core, rows], dst_ref=ag.at[l, core, rows],
            send_sem=cas.at[b, n], recv_sem=car.at[b, n],
            device_id=core_device, device_id_type=MESH,
        )

    def each(first, last, act):
        def step(j, carry):
            act(j)
            return carry

        lax.fori_loop(first, last, step, 0)

    def sum_halves(b):
        l = BATCHES[b][0]
        core_copy(b).wait_recv()

        def chunk(i):
            rows = part(b, plane_to(i))
            psend[l, rows] = (s[l, core, rows] + crecv[l, rows]).astype(BF16)
            plane_copy(b, i).start()

        each(0, 15, chunk)

    def owned(b):
        return z_me - BATCHES[b][3]

    def owns(b):
        return (owned(b) >= 0) & (owned(b) < BATCHES[b][2] // 8)

    def sum_plane(b):
        l, _, chunk, _ = BATCHES[b]

        def add(t, total):
            i = 14 - t
            plane_copy(b, i).wait_recv()
            return total + precv[b, i, pl.ds(0, chunk)].astype(F32)

        rows = part(b, plane_me)
        total = lax.fori_loop(0, 15, add, s[l, core, rows] + crecv[l, rows])
        zsend[b, : chunk // 8] = total.reshape(chunk // 8, 8, 128)

        def send(o):
            @pl.when(owned(b) != o)
            def _():
                z_copy(b, o, z_me).start()

        each(0, chunk // 8, send)

    def sum_z(b):
        @pl.when(owns(b))
        def _():
            o = owned(b)

            def add(t, total):
                sender = (z_me + z_far(14 - t)) % 16
                z_copy(b, o, sender).wait_recv()
                return total + zrecv[b, sender]

            total = lax.fori_loop(0, 15, add, zsend[b, o])
            zfin[b, o] = (total * (1.0 / 512.0)).astype(BF16).astype(F32)
            each(0, 15, lambda i: z_back(b, i, o).start())

    def spread_plane(b):
        l, _, chunk, _ = BATCHES[b]

        def arrive(o):
            @pl.when(owned(b) != o)
            def _():
                z_back(b, 0, o).wait_recv()

        each(0, chunk // 8, arrive)
        ag[l, core, part(b, plane_me)] = zfin[b, : chunk // 8].reshape(chunk, 128).astype(BF16)
        each(0, 15, lambda i: plane_back(b, i).start())
        core_back(b, 15, plane_me).start()

    def out_copy(b, h, n):
        l, base, chunk, _ = BATCHES[b]
        rows = pl.ds(base, min(16 * chunk, HALF - base))
        kernels = pl.ds(base // 64, rows.size // 64)
        return pltpu.make_async_copy(
            ag.reshape(2, 2, 28, 64, 128).at[l, h, kernels], wg.at[l, kernels, h], osem.at[b, n]
        )

    def forward(b):
        def pass_on(t):
            i = 14 - t
            plane_back(b, i).wait_recv()
            core_back(b, i, plane_from(i)).start()

        each(0, 15, pass_on)
        out_copy(b, core, 0).start()

    def finish(b):
        each(0, 16, lambda n: core_back(b, n, plane_me).wait_recv())
        out_copy(b, other, 1).start()

    on = maskv[...] > 0
    g1 = jnp.where(on & (pre[1].astype(F32) > 0), cot[...].astype(F32), 0.0)
    x0 = jnp.where(on, feat[...].astype(F32), 0.0)
    stage_corners(0, g1, x0)
    stage_faces(0, g1)
    pl.semaphore_wait(barrier, 8 + 1 + 2 + 15)
    for group in (0, 1):
        for copy in side_copies(group):
            copy.start()
    stage_faces(1, x0)
    for copy in side_copies(2):
        copy.start()
    relay(0)
    place(0, 0, 0, g1.reshape(64, 8, 128))
    place(1, 0, 0, x0.reshape(64, 8, 128))
    x1 = jnp.where(on, jnp.maximum(pre[0].astype(F32), 0.0), 0.0)
    rowsT[0] = x1.T.astype(BF16)
    for f in (0, 1):
        pg[f, :, 27 * 128 :] = jnp.zeros((512, 128), BF16)

    for group in (0, 1):
        for copy in side_copies(group):
            copy.wait_recv()
    rims(0, 0, 0, 0)
    patches(0, -1)
    kernel_grads(1, 0, 8)
    core_copy(0).start()
    kernel_grads(1, 8, 14)
    core_copy(1).start()
    relayed(0)
    relay(1)
    for copy in w_copies:
        copy.wait()
    d1 = input_grads(1)
    g0 = jnp.where((maskv[...] > 0) & (pre[0].astype(F32) > 0), d1, 0.0).astype(BF16).astype(F32)
    stage_corners(1, g0, g0)
    stage_faces(2, g0)
    for group in (3, 4):
        for copy in side_copies(group):
            copy.start()
    rowsT[1] = g0.T.astype(BF16)
    place(0, 0, 0, g0.reshape(64, 8, 128))
    sum_halves(0)
    sum_halves(1)
    relayed(1)
    relay(2)
    for copy in side_copies(2):
        copy.wait_recv()
    rims(1, 0, 8, 1)
    patches(1, 1)
    kernel_grads(0, 0, 8)
    core_copy(2).start()
    kernel_grads(0, 8, 14)
    core_copy(3).start()
    sum_halves(2)
    sum_halves(3)
    relayed(2)
    sum_plane(0)
    sum_plane(1)
    for group in (3, 4):
        for copy in side_copies(group):
            copy.wait_recv()
    rims(0, 1, 0, 2)
    patches(0, -1)
    d0 = input_grads(0)
    gin[...] = jnp.where(maskv[...] > 0, d0, 0.0).astype(BF16)

    sum_plane(2)
    sum_plane(3)
    for act in (sum_z, spread_plane, forward, finish):
        for b in range(4):
            act(b)

    for group in range(5):
        for copy in side_copies(group):
            copy.wait_send()
    for b in range(4):
        core_copy(b).wait_send()
        core_back(b, 15, plane_me).wait_send()

        def sent(i):
            plane_copy(b, i).wait_send()
            plane_back(b, i).wait_send()
            core_back(b, i, plane_me).wait_send()

        each(0, 15, sent)

        def sent_z(o):
            @pl.when(owned(b) != o)
            def _():
                z_copy(b, o, z_me).wait_send()

        each(0, BATCHES[b][2] // 8, sent_z)

        @pl.when(owns(b))
        def _():
            each(0, 15, lambda i: z_back(b, i, owned(b)).wait_send())

        out_copy(b, core, 0).wait()
        out_copy(b, other, 1).wait()


def on_device(features, pre_acts, cotangent, weights, voxel_mask, neighbours):
    vmem = pl.BlockSpec(memory_space=pltpu.VMEM)
    anywhere = pl.BlockSpec(memory_space=pl.ANY)
    dma = pltpu.SemaphoreType.DMA
    gin, wg = pl.pallas_call(
        kernel,
        out_shape=(
            jax.ShapeDtypeStruct((512, 128), BF16),
            jax.ShapeDtypeStruct((2, 27, 2, 64, 128), BF16),
        ),
        in_specs=[anywhere] * 6,
        out_specs=(vmem, anywhere),
        scratch_shapes=[
            pltpu.VMEM((512, 128), BF16),
            pltpu.VMEM((2, 512, 128), BF16),
            pltpu.VMEM((512, 128), BF16),
            pltpu.VMEM((1, 512), jnp.int32),
            pltpu.SMEM((1, 27), jnp.int32),
            pltpu.VMEM((2, 27, 128, 128), BF16),
            pltpu.VMEM((512, 128), F32),
            pltpu.VMEM((2, 3, 10, 10, 8, 128), F32),
            pltpu.VMEM((2, 512, 28 * 128), BF16),
            pltpu.VMEM((2, 128, 512), BF16),
            pltpu.VMEM((3, 4, 64, 128), BF16),
            pltpu.VMEM((2, 4, 16, 128), BF16),
            pltpu.VMEM((3, 4, 64, 128), BF16),
            pltpu.VMEM((2, 4, 16, 128), BF16),
            pltpu.VMEM((2, 2, 28 * 64, 128), F32),
            pltpu.VMEM((2, 28 * 64, 128), F32),
            pltpu.VMEM((2, 28 * 64, 128), BF16),
            pltpu.VMEM((4, 15, 64, 128), BF16),
            pltpu.VMEM((4, 8, 8, 128), F32),
            pltpu.VMEM((4, 16, 8, 128), F32),
            pltpu.VMEM((4, 8, 8, 128), F32),
            pltpu.VMEM((2, 2, 28 * 64, 128), BF16),
            dma((5,)), dma((2,)), dma((4, 2)), dma((5, 4)), dma((5, 4)), dma((4,)), dma((4,)),
            dma((4, 15)), dma((4, 15)), dma((4, 8)), dma((4, 16)), dma((4, 15)), dma((4, 8)),
            dma((4, 15)), dma((4, 15)), dma((4, 16)), dma((4, 16)), pltpu.SemaphoreType.REGULAR((3,)),
        ],
        compiler_params=pltpu.CompilerParams(
            collective_id=0, has_side_effects=True, vmem_limit_bytes=40 * 1024 * 1024
        ),
        cost_estimate=pl.CostEstimate(flops=2_000_000_000, bytes_accessed=5_000_000, transcendentals=0),
    )(
        *(
            pltpu.with_memory_space_constraint(v, pltpu.HBM)
            for v in (
                features.reshape(512, 128),
                pre_acts.reshape(2, 512, 128),
                cotangent.reshape(512, 128),
                voxel_mask.reshape(1, 512),
                neighbours.reshape(1, 27),
                weights,
            )
        )
    )
    return gin.reshape(1, 1, 1, 8, 8, 8, 128), wg.reshape(2, 27, 128, 128)


def solution(mesh):
    in_specs = (
        P("gx", "gy", None, None, None, None, None),
        P(None, "gx", "gy", None, None, None, None, None),
        P("gx", "gy", None, None, None, None, None),
        P(),
        P("gx", "gy", None, None),
        P("gx", "gy", None, None),
    )
    out_specs = (P("gx", "gy", None, None, None, None, None), P())
    return jax.shard_map(
        on_device, mesh=mesh, in_specs=in_specs, out_specs=out_specs, check_vma=False
    )
```

```python
import jax
import jax.numpy as jnp
from jax import lax
from jax.experimental import pallas as pl
from jax.experimental.pallas import tpu as pltpu
from jax.sharding import PartitionSpec as P

F32 = jnp.float32
BF16 = jnp.bfloat16
MESH = pl.DeviceIdType.MESH
SIDES = [(a, b) for a in (-1, 0, 1) for b in (-1, 0, 1) if (a, b) != (0, 0)]
BATCHES = ((1, 0, 64), (1, 1024, 48), (0, 0, 64), (0, 1024, 48))
HALF = 27 * 64


def kernel(
    feat_any, pre_any, cot_any, mask_any, nbr_any, w_any, gin, wg,
    feat, pre, cot, mask, nbr, wv, maskv, pad, pg, rowsT, gface, gcorner, rface, rcorner,
    s, crecv, psend, precv, zrecv, ag,
    isem, wsem, osem, hss, hrs, css, crs, pss, prs, zss, zrs, pas, par, cas, car, relays,
):
    gx, gy = lax.axis_index("gx"), lax.axis_index("gy")
    z_hi, x = gx // 4, gx % 4
    y, z_lo, core = gy // 8, (gy // 2) % 4, gy % 2
    other = 1 - core
    plane_me = x * 4 + y
    member, place_z = z_lo % 2, z_hi * 2 + z_lo // 2

    def plane_device(i, m):
        return {"gx": z_hi * 4 + i // 4, "gy": (i % 4) * 8 + (z_lo - member + m) * 2 + core}

    def z_device(i):
        return {"gx": (i // 2) * 4 + x, "gy": y * 8 + ((i % 2) * 2 + member) * 2 + core}

    partner = {"gx": gx, "gy": gy + 2 - 4 * member}
    core_device = {"gx": gx, "gy": gy + 1 - 2 * core}

    def side_device(a, b):
        return {"gx": (gx + a + 16) % 16, "gy": (gy + b + 32) % 32}

    def plane_shift(i):
        v = i + i // 10
        return (2 + v // 4) % 4, (2 + v % 4) % 4

    def plane_to(i):
        dx, dy = plane_shift(i)
        return ((x + dx) % 4) * 4 + (y + dy) % 4

    def plane_from(i):
        dx, dy = plane_shift(i)
        return ((x + 4 - dx) % 4) * 4 + (y + 4 - dy) % 4

    def z_far(i):
        return 4 + (i // 2) - (i % 2) * (2 * (i // 2) + 1)

    inputs = [
        pltpu.make_async_copy(src, dst, isem.at[n])
        for n, (src, dst) in enumerate(
            ((mask_any, mask), (nbr_any, nbr), (cot_any, cot), (pre_any, pre), (feat_any, feat))
        )
    ]
    for copy in inputs:
        copy.start()

    barrier = pltpu.get_barrier_semaphore()

    def greet(sem, device):
        pl.semaphore_signal(sem, inc=1, device_id=device, device_id_type=MESH)

    def relay(step):
        for shift in (2**step, 8 - 2**step):
            greet(relays.at[step], z_device((place_z + shift) % 8))

    def relayed(step):
        pl.semaphore_wait(relays.at[step], 2)

    for a, b in SIDES:
        greet(barrier, side_device(a, b))
    greet(barrier, core_device)
    greet(barrier, partner)
    for shift in (1, 7):
        greet(barrier, z_device((place_z + shift) % 8))

    def greet_plane(i, carry):
        for m in (0, 1):
            greet(barrier, plane_device(plane_to(i), m))
        return carry

    lax.fori_loop(0, 15, greet_plane, 0)
    w_copies = [pltpu.make_async_copy(w_any.at[l], wv.at[l], wsem.at[l]) for l in (1, 0)]
    for copy in w_copies:
        copy.start()

    for copy in inputs:
        copy.wait()
    rows = lax.broadcasted_iota(jnp.int32, (128, 128), 0)
    cols = lax.broadcasted_iota(jnp.int32, (128, 128), 1)
    ones = jnp.ones((128, 128), BF16)
    for r in range(4):
        line = (mask[:, r * 128 : (r + 1) * 128] > 0).astype(F32)
        spread = jnp.where(rows == cols, jnp.broadcast_to(line, (128, 128)), 0.0).astype(BF16)
        maskv[r * 128 : (r + 1) * 128] = jnp.dot(spread, ones, preferred_element_type=F32)

    def flag(a, b, c):
        return jnp.where(nbr[0, (a + 1) * 9 + (b + 1) * 3 + c + 1] >= 0, 1.0, 0.0)

    level = lax.broadcasted_iota(jnp.int32, (1, 8, 128), 1)

    def place(f, a, b, tile):
        low, mid, high = flag(a, b, -1), flag(a, b, 0), flag(a, b, 1)
        nx, ny = (1 if a else 8), (1 if b else 8)
        x0, y0 = {-1: 0, 0: 1, 1: 9}[a], {-1: 0, 0: 1, 1: 9}[b]
        shape = (nx, ny, 8, 128)
        below = pltpu.roll(tile, 1, 1) * jnp.where(level == 0, low, mid)
        above = pltpu.roll(tile, 7, 1) * jnp.where(level == 7, high, mid)
        pad[f, 0, x0 : x0 + nx, y0 : y0 + ny] = below.reshape(shape)
        pad[f, 1, x0 : x0 + nx, y0 : y0 + ny] = (tile * mid).reshape(shape)
        pad[f, 2, x0 : x0 + nx, y0 : y0 + ny] = above.reshape(shape)

    def side_copies(group):
        copies = []
        for a, b in SIDES:
            if (group in (0, 3)) != bool(a and b):
                continue
            if a and b:
                i, j = (a + 1) + (b + 1) // 2, (1 - a) + (1 - b) // 2
                src, dst = gcorner.at[group // 3, i], rcorner.at[group // 3, j]
            else:
                i = (a + 1) // 2 if a else 2 + (b + 1) // 2
                j = (1 - a) // 2 if a else 2 + (1 - b) // 2
                face = {1: 0, 2: 1, 4: 2}[group]
                src, dst = gface.at[face, i], rface.at[face, j]
            copies.append(
                pltpu.make_async_remote_copy(
                    src_ref=src, dst_ref=dst, send_sem=hss.at[group, i], recv_sem=hrs.at[group, j],
                    device_id=side_device(a, b), device_id_type=MESH,
                )
            )
        return copies

    def stage_corners(n, first, second):
        for i in (0, 1):
            for j in (0, 1):
                cells = [v.reshape(8, 8, 8, 128)[7 * i, 7 * j] for v in (first, second)]
                gcorner[n, 2 * i + j] = jnp.concatenate(cells, axis=0).astype(BF16)

    def stage_faces(n, v):
        v4 = v.reshape(8, 8, 8, 128)
        for i in (0, 1):
            gface[n, i] = v4[7 * i].reshape(64, 128).astype(BF16)
            gface[n, 2 + i] = v4[:, 7 * i].reshape(64, 128).astype(BF16)

    def rims(f, corners, row, face):
        for a, b in SIDES:
            if a and b:
                cell = rcorner[corners, (a + 1) + (b + 1) // 2].astype(F32)[row : row + 8]
                place(f, a, b, cell.reshape(1, 8, 128))
            else:
                i = (a + 1) // 2 if a else 2 + (b + 1) // 2
                place(f, a, b, rface[face, i].astype(F32).reshape(8, 8, 128))

    def patches(f, sign):
        for k in range(27):
            a, b, c = (sign * v for v in (k // 9 - 1, (k // 3) % 3 - 1, k % 3 - 1))
            window = pad[f, 1 + c, 1 + a : 9 + a, 1 + b : 9 + b]
            pg[f, :, k * 128 : (k + 1) * 128] = window.reshape(512, 128).astype(BF16)

    def input_grads(l):
        kernels = jnp.concatenate([wv[l, k] for k in range(27)], axis=1)
        return lax.dot_general(
            pg[0, :, : 27 * 128], kernels, (((1,), (1,)), ((), ())), preferred_element_type=F32
        )

    def kernel_grads(l, first, last):
        f = 1 - l
        for m in range(first, last):
            both = jnp.dot(
                rowsT[f], pg[f, :, m * 256 : (m + 1) * 256], preferred_element_type=F32
            )
            for q in (0, 1):
                block = both[:, q * 128 : (q + 1) * 128]
                block = block.T if l == 0 else block
                for h in (0, 1):
                    at = m * 128 + q * 64
                    s[l, h, at : at + 64] = block[h * 64 : (h + 1) * 64]

    def part(b, i):
        _, base, chunk = BATCHES[b]
        return pl.ds(pl.multiple_of(base + i * chunk, 16), chunk)

    def piece(b, i, m, n):
        _, base, chunk = BATCHES[b]
        return pl.ds(pl.multiple_of(base + i * chunk + 32 * m, 16), n)

    def by_member(b, act):
        sizes = (32, BATCHES[b][2] - 32)
        if sizes[0] == sizes[1]:
            act(member, *sizes)
            return
        for m in (0, 1):

            @pl.when(member == m)
            def _():
                act(m, sizes[m], sizes[1 - m])

    def core_copy(b):
        l, base, chunk = BATCHES[b]
        rows = pl.ds(base, 16 * chunk)
        return pltpu.make_async_remote_copy(
            src_ref=s.at[l, other, rows], dst_ref=crecv.at[l, rows],
            send_sem=css.at[b], recv_sem=crs.at[b],
            device_id=core_device, device_id_type=MESH,
        )

    def plane_copy(b, i, m, n):
        peer = plane_to(i)
        return pltpu.make_async_remote_copy(
            src_ref=psend.at[BATCHES[b][0], piece(b, peer, m, n)],
            dst_ref=precv.at[b, 2 * i + member, pl.ds(0, n)],
            send_sem=pss.at[b, 2 * i + m], recv_sem=prs.at[b, 2 * i + member],
            device_id=plane_device(peer, m), device_id_type=MESH,
        )

    def pair_copy(b, m, n):
        return pltpu.make_async_remote_copy(
            src_ref=psend.at[BATCHES[b][0], piece(b, plane_me, m, n)],
            dst_ref=precv.at[b, 30, pl.ds(0, n)],
            send_sem=pss.at[b, 30], recv_sem=prs.at[b, 30],
            device_id=partner, device_id_type=MESH,
        )

    def plane_arrival(b, slot, n):
        rows = precv.at[b, slot, pl.ds(0, n)]
        return pltpu.make_async_remote_copy(
            src_ref=rows, dst_ref=rows, send_sem=pss.at[b, slot], recv_sem=prs.at[b, slot],
            device_id=partner, device_id_type=MESH,
        )

    def z_copy(b, i, n):
        rows = zrecv.at[b, place_z, pl.ds(0, n)]
        return pltpu.make_async_remote_copy(
            src_ref=rows, dst_ref=rows, send_sem=zss.at[b, i], recv_sem=zrs.at[b, place_z],
            device_id=z_device((place_z + z_far(i)) % 8), device_id_type=MESH,
        )

    def z_arrival(b, i, n):
        sender = (place_z + z_far(i)) % 8
        rows = zrecv.at[b, sender, pl.ds(0, n)]
        return pltpu.make_async_remote_copy(
            src_ref=rows, dst_ref=rows, send_sem=zss.at[b, i], recv_sem=zrs.at[b, sender],
            device_id=partner, device_id_type=MESH,
        )

    def plane_back(b, i, to, m, n):
        rows = ag.at[BATCHES[b][0], core, piece(b, plane_me, m, n)]
        return pltpu.make_async_remote_copy(
            src_ref=rows, dst_ref=rows,
            send_sem=pas.at[b, 2 * i + to], recv_sem=par.at[b, 2 * i + member],
            device_id=plane_device(plane_to(i), to), device_id_type=MESH,
        )

    def plane_return(b, i, m, n):
        rows = ag.at[BATCHES[b][0], core, piece(b, plane_from(i), m, n)]
        return pltpu.make_async_remote_copy(
            src_ref=rows, dst_ref=rows,
            send_sem=pas.at[b, 2 * i + m], recv_sem=par.at[b, 2 * i + m],
            device_id=partner, device_id_type=MESH,
        )

    def pair_back(b, m, n):
        rows = ag.at[BATCHES[b][0], core, piece(b, plane_me, m, n)]
        return pltpu.make_async_remote_copy(
            src_ref=rows, dst_ref=rows, send_sem=pas.at[b, 30], recv_sem=par.at[b, 30],
            device_id=partner, device_id_type=MESH,
        )

    def core_back(b, n, owner):
        l = BATCHES[b][0]
        rows = part(b, owner)
        return pltpu.make_async_remote_copy(
            src_ref=ag.at[l, core, rows], dst_ref=ag.at[l, core, rows],
            send_sem=cas.at[b, n], recv_sem=car.at[b, n],
            device_id=core_device, device_id_type=MESH,
        )

    def each(first, last, act):
        def step(j, carry):
            act(j)
            return carry

        lax.fori_loop(first, last, step, 0)

    def sum_halves(b):
        l, _, size = BATCHES[b]
        core_copy(b).wait_recv()

        def chunk(i):
            rows = part(b, plane_to(i))
            psend[l, rows] = (s[l, core, rows] + crecv[l, rows]).astype(BF16)
            plane_copy(b, i, 0, 32).start()
            plane_copy(b, i, 1, size - 32).start()

        each(0, 15, chunk)
        rows = part(b, plane_me)
        psend[l, rows] = (s[l, core, rows] + crecv[l, rows]).astype(BF16)
        by_member(b, lambda m, n, k: pair_copy(b, 1 - m, k).start())

    def sum_plane(b):
        l = BATCHES[b][0]

        def total_of(m, n, k):
            def add(t, total):
                plane_arrival(b, 30 - t, n).wait_recv()
                return total + precv[b, 30 - t, pl.ds(0, n)].astype(F32)

            rows = piece(b, plane_me, m, n)
            total = lax.fori_loop(0, 31, add, s[l, core, rows] + crecv[l, rows])
            zrecv[b, place_z, pl.ds(0, n)] = total.astype(BF16)
            each(0, 7, lambda i: z_copy(b, i, n).start())

        by_member(b, total_of)

    def sum_z(b):
        l = BATCHES[b][0]

        def total_of(m, n, k):
            each(0, 7, lambda i: z_arrival(b, 6 - i, n).wait_recv())

            def add(q, total):
                return total + zrecv[b, q, pl.ds(0, n)].astype(F32)

            total = lax.fori_loop(0, 8, add, jnp.zeros((n, 128), F32))
            ag[l, core, piece(b, plane_me, m, n)] = (total * (1.0 / 512.0)).astype(BF16)

            def send(i):
                plane_back(b, i, 0, m, n).start()
                plane_back(b, i, 1, m, n).start()

            each(0, 15, send)
            pair_back(b, m, n).start()

        by_member(b, total_of)

    def out_copy(b, h, n):
        l, base, chunk = BATCHES[b]
        rows = pl.ds(base, min(16 * chunk, HALF - base))
        kernels = pl.ds(base // 64, rows.size // 64)
        return pltpu.make_async_copy(
            ag.reshape(2, 2, 28, 64, 128).at[l, h, kernels], wg.at[l, kernels, h], osem.at[b, n]
        )

    def forward(b):
        def pass_on(t):
            i = 14 - t
            plane_return(b, i, 0, 32).wait_recv()
            plane_return(b, i, 1, BATCHES[b][2] - 32).wait_recv()
            core_back(b, i, plane_from(i)).start()

        by_member(b, lambda m, n, k: pair_back(b, 1 - m, k).wait_recv())
        core_back(b, 15, plane_me).start()
        each(0, 15, pass_on)
        out_copy(b, core, 0).start()

    def finish(b):
        each(0, 16, lambda n: core_back(b, n, plane_me).wait_recv())
        out_copy(b, other, 1).start()

    on = maskv[...] > 0
    g1 = jnp.where(on & (pre[1].astype(F32) > 0), cot[...].astype(F32), 0.0)
    x0 = jnp.where(on, feat[...].astype(F32), 0.0)
    stage_corners(0, g1, x0)
    stage_faces(0, g1)
    pl.semaphore_wait(barrier, 8 + 1 + 1 + 2 + 30)
    for group in (0, 1):
        for copy in side_copies(group):
            copy.start()
    stage_faces(1, x0)
    for copy in side_copies(2):
        copy.start()
    relay(0)
    place(0, 0, 0, g1.reshape(64, 8, 128))
    place(1, 0, 0, x0.reshape(64, 8, 128))
    x1 = jnp.where(on, jnp.maximum(pre[0].astype(F32), 0.0), 0.0)
    rowsT[0] = x1.T.astype(BF16)
    for f in (0, 1):
        pg[f, :, 27 * 128 :] = jnp.zeros((512, 128), BF16)

    for group in (0, 1):
        for copy in side_copies(group):
            copy.wait_recv()
    rims(0, 0, 0, 0)
    patches(0, -1)
    kernel_grads(1, 0, 8)
    core_copy(0).start()
    kernel_grads(1, 8, 14)
    core_copy(1).start()
    relayed(0)
    relay(1)
    for copy in w_copies:
        copy.wait()
    d1 = input_grads(1)
    g0 = jnp.where((maskv[...] > 0) & (pre[0].astype(F32) > 0), d1, 0.0).astype(BF16).astype(F32)
    stage_corners(1, g0, g0)
    stage_faces(2, g0)
    for group in (3, 4):
        for copy in side_copies(group):
            copy.start()
    rowsT[1] = g0.T.astype(BF16)
    place(0, 0, 0, g0.reshape(64, 8, 128))
    sum_halves(0)
    sum_halves(1)
    for copy in side_copies(2):
        copy.wait_recv()
    rims(1, 0, 8, 1)
    patches(1, 1)
    kernel_grads(0, 0, 8)
    core_copy(2).start()
    kernel_grads(0, 8, 14)
    core_copy(3).start()
    sum_halves(2)
    sum_halves(3)
    relayed(1)
    sum_plane(0)
    sum_plane(1)
    for group in (3, 4):
        for copy in side_copies(group):
            copy.wait_recv()
    rims(0, 1, 0, 2)
    patches(0, -1)
    d0 = input_grads(0)
    gin[...] = jnp.where(maskv[...] > 0, d0, 0.0).astype(BF16)

    sum_plane(2)
    sum_plane(3)
    for act in (sum_z, forward, finish):
        for b in range(4):
            act(b)

    for group in range(5):
        for copy in side_copies(group):
            copy.wait_send()
    for b in range(4):
        core_copy(b).wait_send()
        core_back(b, 15, plane_me).wait_send()

        def sent(i):
            plane_copy(b, i, 0, 32).wait_send()
            plane_copy(b, i, 1, BATCHES[b][2] - 32).wait_send()
            core_back(b, i, plane_me).wait_send()

        each(0, 15, sent)

        def sent_own(m, n, k):
            pair_copy(b, 1 - m, k).wait_send()
            pair_back(b, m, n).wait_send()
            each(0, 7, lambda i: z_copy(b, i, n).wait_send())

            def sent_back(i):
                plane_back(b, i, 0, m, n).wait_send()
                plane_back(b, i, 1, m, n).wait_send()

            each(0, 15, sent_back)

        by_member(b, sent_own)
        out_copy(b, core, 0).wait()
        out_copy(b, other, 1).wait()


def on_device(features, pre_acts, cotangent, weights, voxel_mask, neighbours):
    vmem = pl.BlockSpec(memory_space=pltpu.VMEM)
    anywhere = pl.BlockSpec(memory_space=pl.ANY)
    dma = pltpu.SemaphoreType.DMA
    gin, wg = pl.pallas_call(
        kernel,
        out_shape=(
            jax.ShapeDtypeStruct((512, 128), BF16),
            jax.ShapeDtypeStruct((2, 27, 2, 64, 128), BF16),
        ),
        in_specs=[anywhere] * 6,
        out_specs=(vmem, anywhere),
        scratch_shapes=[
            pltpu.VMEM((512, 128), BF16),
            pltpu.VMEM((2, 512, 128), BF16),
            pltpu.VMEM((512, 128), BF16),
            pltpu.VMEM((1, 512), jnp.int32),
            pltpu.SMEM((1, 27), jnp.int32),
            pltpu.VMEM((2, 27, 128, 128), BF16),
            pltpu.VMEM((512, 128), F32),
            pltpu.VMEM((2, 3, 10, 10, 8, 128), F32),
            pltpu.VMEM((2, 512, 28 * 128), BF16),
            pltpu.VMEM((2, 128, 512), BF16),
            pltpu.VMEM((3, 4, 64, 128), BF16),
            pltpu.VMEM((2, 4, 16, 128), BF16),
            pltpu.VMEM((3, 4, 64, 128), BF16),
            pltpu.VMEM((2, 4, 16, 128), BF16),
            pltpu.VMEM((2, 2, 28 * 64, 128), F32),
            pltpu.VMEM((2, 28 * 64, 128), F32),
            pltpu.VMEM((2, 28 * 64, 128), BF16),
            pltpu.VMEM((4, 31, 32, 128), BF16),
            pltpu.VMEM((4, 8, 32, 128), BF16),
            pltpu.VMEM((2, 2, 28 * 64, 128), BF16),
            dma((5,)), dma((2,)), dma((4, 2)), dma((5, 4)), dma((5, 4)), dma((4,)), dma((4,)),
            dma((4, 31)), dma((4, 31)), dma((4, 7)), dma((4, 8)),
            dma((4, 31)), dma((4, 31)), dma((4, 16)), dma((4, 16)), pltpu.SemaphoreType.REGULAR((2,)),
        ],
        compiler_params=pltpu.CompilerParams(
            collective_id=0, has_side_effects=True, vmem_limit_bytes=40 * 1024 * 1024
        ),
        cost_estimate=pl.CostEstimate(flops=2_000_000_000, bytes_accessed=5_000_000, transcendentals=0),
    )(
        *(
            pltpu.with_memory_space_constraint(v, pltpu.HBM)
            for v in (
                features.reshape(512, 128),
                pre_acts.reshape(2, 512, 128),
                cotangent.reshape(512, 128),
                voxel_mask.reshape(1, 512),
                neighbours.reshape(1, 27),
                weights,
            )
        )
    )
    return gin.reshape(1, 1, 1, 8, 8, 8, 128), wg.reshape(2, 27, 128, 128)


def solution(mesh):
    in_specs = (
        P("gx", "gy", None, None, None, None, None),
        P(None, "gx", "gy", None, None, None, None, None),
        P("gx", "gy", None, None, None, None, None),
        P(),
        P("gx", "gy", None, None),
        P("gx", "gy", None, None),
    )
    out_specs = (P("gx", "gy", None, None, None, None, None), P())
    return jax.shard_map(
        on_device, mesh=mesh, in_specs=in_specs, out_specs=out_specs, check_vma=False
    )
```

```python
import jax
import jax.numpy as jnp
from jax import lax
from jax.experimental import pallas as pl
from jax.experimental.pallas import tpu as pltpu
from jax.sharding import PartitionSpec as P

F32 = jnp.float32
BF16 = jnp.bfloat16
MESH = pl.DeviceIdType.MESH
SIDES = [(a, b) for a in (-1, 0, 1) for b in (-1, 0, 1) if (a, b) != (0, 0)]
BATCHES = ((1, 0, 64, 0), (1, 1024, 48, 2), (0, 0, 64, 1), (0, 1024, 48, 3))
HALF = 27 * 64


def kernel(
    feat_any, pre_any, cot_any, mask_any, nbr_any, w_any, gin, wg,
    feat, pre, cot, mask, nbr, wv, maskv, pad, pg, rowsT, gface, gcorner, rface, rcorner,
    s, crecv, psend, precv, zsend, zrecv, zfin, ag,
    isem, wsem, osem, hss, hrs, css, crs, pss, prs, zss, zrs, zas, zar, pas, par, cas, car, relays,
):
    gx, gy = lax.axis_index("gx"), lax.axis_index("gy")
    z_hi, x = gx // 4, gx % 4
    y, z_lo, core = gy // 8, (gy // 2) % 4, gy % 2
    other = 1 - core
    plane_me = x * 4 + y
    z_me = z_hi * 4 + z_lo

    def plane_device(i):
        return {"gx": z_hi * 4 + i // 4, "gy": (i % 4) * 8 + z_lo * 2 + core}

    def z_device(i):
        return {"gx": (i // 4) * 4 + x, "gy": y * 8 + (i % 4) * 2 + core}

    core_device = {"gx": gx, "gy": gy + 1 - 2 * core}

    def side_device(a, b):
        return {"gx": (gx + a + 16) % 16, "gy": (gy + b + 32) % 32}

    def plane_shift(i):
        v = i + i // 10
        return (2 + v // 4) % 4, (2 + v % 4) % 4

    def plane_to(i):
        dx, dy = plane_shift(i)
        return ((x + dx) % 4) * 4 + (y + dy) % 4

    def plane_from(i):
        dx, dy = plane_shift(i)
        return ((x + 4 - dx) % 4) * 4 + (y + 4 - dy) % 4

    def z_far(i):
        return 8 + (i // 2) - (i % 2) * (2 * (i // 2) + 1)

    inputs = [
        pltpu.make_async_copy(src, dst, isem.at[n])
        for n, (src, dst) in enumerate(
            ((mask_any, mask), (nbr_any, nbr), (cot_any, cot), (pre_any, pre), (feat_any, feat))
        )
    ]
    for copy in inputs:
        copy.start()

    barrier = pltpu.get_barrier_semaphore()

    def greet(sem, device):
        pl.semaphore_signal(sem, inc=1, device_id=device, device_id_type=MESH)

    def relay(step):
        for shift in (2**step, 16 - 2**step):
            greet(relays.at[step], z_device((z_me + shift) % 16))

    def relayed(step):
        pl.semaphore_wait(relays.at[step], 2)

    for a, b in SIDES:
        greet(barrier, side_device(a, b))
    greet(barrier, core_device)
    for shift in (1, 15):
        greet(barrier, z_device((z_me + shift) % 16))

    def greet_plane(i, carry):
        greet(barrier, plane_device(plane_to(i)))
        return carry

    lax.fori_loop(0, 15, greet_plane, 0)
    w_copies = [pltpu.make_async_copy(w_any.at[l], wv.at[l], wsem.at[l]) for l in (1, 0)]
    for copy in w_copies:
        copy.start()

    for copy in inputs:
        copy.wait()
    rows = lax.broadcasted_iota(jnp.int32, (128, 128), 0)
    cols = lax.broadcasted_iota(jnp.int32, (128, 128), 1)
    ones = jnp.ones((128, 128), BF16)
    for r in range(4):
        line = (mask[:, r * 128 : (r + 1) * 128] > 0).astype(F32)
        spread = jnp.where(rows == cols, jnp.broadcast_to(line, (128, 128)), 0.0).astype(BF16)
        maskv[r * 128 : (r + 1) * 128] = jnp.dot(spread, ones, preferred_element_type=F32)

    def flag(a, b, c):
        return jnp.where(nbr[0, (a + 1) * 9 + (b + 1) * 3 + c + 1] >= 0, 1.0, 0.0)

    level = lax.broadcasted_iota(jnp.int32, (1, 8, 128), 1)

    def place(f, a, b, tile):
        low, mid, high = flag(a, b, -1), flag(a, b, 0), flag(a, b, 1)
        nx, ny = (1 if a else 8), (1 if b else 8)
        x0, y0 = {-1: 0, 0: 1, 1: 9}[a], {-1: 0, 0: 1, 1: 9}[b]
        shape = (nx, ny, 8, 128)
        below = pltpu.roll(tile, 1, 1) * jnp.where(level == 0, low, mid)
        above = pltpu.roll(tile, 7, 1) * jnp.where(level == 7, high, mid)
        pad[f, 0, x0 : x0 + nx, y0 : y0 + ny] = below.reshape(shape)
        pad[f, 1, x0 : x0 + nx, y0 : y0 + ny] = (tile * mid).reshape(shape)
        pad[f, 2, x0 : x0 + nx, y0 : y0 + ny] = above.reshape(shape)

    def side_copies(group):
        copies = []
        for a, b in SIDES:
            if (group in (0, 3)) != bool(a and b):
                continue
            if a and b:
                i, j = (a + 1) + (b + 1) // 2, (1 - a) + (1 - b) // 2
                src, dst = gcorner.at[group // 3, i], rcorner.at[group // 3, j]
            else:
                i = (a + 1) // 2 if a else 2 + (b + 1) // 2
                j = (1 - a) // 2 if a else 2 + (1 - b) // 2
                face = {1: 0, 2: 1, 4: 2}[group]
                src, dst = gface.at[face, i], rface.at[face, j]
            copies.append(
                pltpu.make_async_remote_copy(
                    src_ref=src, dst_ref=dst, send_sem=hss.at[group, i], recv_sem=hrs.at[group, j],
                    device_id=side_device(a, b), device_id_type=MESH,
                )
            )
        return copies

    def stage_corners(n, first, second):
        for i in (0, 1):
            for j in (0, 1):
                cells = [v.reshape(8, 8, 8, 128)[7 * i, 7 * j] for v in (first, second)]
                gcorner[n, 2 * i + j] = jnp.concatenate(cells, axis=0).astype(BF16)

    def stage_faces(n, v):
        v4 = v.reshape(8, 8, 8, 128)
        for i in (0, 1):
            gface[n, i] = v4[7 * i].reshape(64, 128).astype(BF16)
            gface[n, 2 + i] = v4[:, 7 * i].reshape(64, 128).astype(BF16)

    def rims(f, corners, row, face):
        for a, b in SIDES:
            if a and b:
                cell = rcorner[corners, (a + 1) + (b + 1) // 2].astype(F32)[row : row + 8]
                place(f, a, b, cell.reshape(1, 8, 128))
            else:
                i = (a + 1) // 2 if a else 2 + (b + 1) // 2
                place(f, a, b, rface[face, i].astype(F32).reshape(8, 8, 128))

    def patches(f, sign):
        for k in range(27):
            a, b, c = (sign * v for v in (k // 9 - 1, (k // 3) % 3 - 1, k % 3 - 1))
            window = pad[f, 1 + c, 1 + a : 9 + a, 1 + b : 9 + b]
            pg[f, :, k * 128 : (k + 1) * 128] = window.reshape(512, 128).astype(BF16)

    def input_grads(l):
        kernels = jnp.concatenate([wv[l, k] for k in range(27)], axis=1)
        return lax.dot_general(
            pg[0, :, : 27 * 128], kernels, (((1,), (1,)), ((), ())), preferred_element_type=F32
        )

    def kernel_grads(l, first, last):
        f = 1 - l
        for m in range(first, last):
            both = jnp.dot(
                rowsT[f], pg[f, :, m * 256 : (m + 1) * 256], preferred_element_type=F32
            )
            for q in (0, 1):
                block = both[:, q * 128 : (q + 1) * 128]
                block = block.T if l == 0 else block
                for h in (0, 1):
                    at = m * 128 + q * 64
                    s[l, h, at : at + 64] = block[h * 64 : (h + 1) * 64]

    def part(b, i):
        _, base, chunk, _ = BATCHES[b]
        return pl.ds(pl.multiple_of(base + i * chunk, 16), chunk)

    def core_copy(b):
        l, base, chunk, _ = BATCHES[b]
        rows = pl.ds(base, 16 * chunk)
        return pltpu.make_async_remote_copy(
            src_ref=s.at[l, other, rows], dst_ref=crecv.at[l, rows],
            send_sem=css.at[b], recv_sem=crs.at[b],
            device_id=core_device, device_id_type=MESH,
        )

    def plane_copy(b, i):
        l, _, chunk, _ = BATCHES[b]
        peer = plane_to(i)
        return pltpu.make_async_remote_copy(
            src_ref=psend.at[l, part(b, peer)], dst_ref=precv.at[b, i, pl.ds(0, chunk)],
            send_sem=pss.at[b], recv_sem=prs.at[b],
            device_id=plane_device(peer), device_id_type=MESH,
        )

    def z_copy(b, o):
        owner = BATCHES[b][3] + 4 * o
        return pltpu.make_async_remote_copy(
            src_ref=zsend.at[b, o], dst_ref=zrecv.at[b, (owner + 15 - z_me) % 16],
            send_sem=zss.at[b, o], recv_sem=zrs.at[b],
            device_id=z_device(owner), device_id_type=MESH,
        )

    def bytes_of(ref, send_sem, recv_sem):
        return pltpu.make_async_remote_copy(
            src_ref=ref, dst_ref=ref, send_sem=send_sem, recv_sem=recv_sem,
            device_id=core_device, device_id_type=MESH,
        )

    def plane_all(b):
        return bytes_of(precv.at[b, :, pl.ds(0, BATCHES[b][2])], pss.at[b], prs.at[b])

    def z_all(b):
        return bytes_of(zrecv.at[b], zas.at[b], zrs.at[b])

    def back_all(b, count, send_sem, recv_sem):
        l, base, chunk, _ = BATCHES[b]
        return bytes_of(ag.at[l, core, pl.ds(base, count * chunk)], send_sem, recv_sem)

    def z_back(b, i, o):
        return pltpu.make_async_remote_copy(
            src_ref=zfin.at[b, o], dst_ref=zfin.at[b, o],
            send_sem=zas.at[b], recv_sem=zar.at[b, o],
            device_id=z_device((z_me + z_far(i)) % 16), device_id_type=MESH,
        )

    def plane_back(b, i):
        l = BATCHES[b][0]
        rows = part(b, plane_me)
        return pltpu.make_async_remote_copy(
            src_ref=ag.at[l, core, rows], dst_ref=ag.at[l, core, rows],
            send_sem=pas.at[b], recv_sem=par.at[b, i],
            device_id=plane_device(plane_to(i)), device_id_type=MESH,
        )

    def core_back(b, owner):
        l = BATCHES[b][0]
        rows = part(b, owner)
        return pltpu.make_async_remote_copy(
            src_ref=ag.at[l, core, rows], dst_ref=ag.at[l, core, rows],
            send_sem=cas.at[b], recv_sem=car.at[b],
            device_id=core_device, device_id_type=MESH,
        )

    def each(first, last, act):
        def step(j, carry):
            act(j)
            return carry

        lax.fori_loop(first, last, step, 0)

    def sum_halves(b):
        l = BATCHES[b][0]
        core_copy(b).wait_recv()

        def chunk(i):
            rows = part(b, plane_to(i))
            psend[l, rows] = (s[l, core, rows] + crecv[l, rows]).astype(BF16)
            plane_copy(b, i).start()

        each(0, 15, chunk)

    def mine(b, o):
        return (z_lo == BATCHES[b][3]) & (z_hi == o)

    def owns(b):
        return (z_lo == BATCHES[b][3]) & (z_hi < BATCHES[b][2] // 16)

    def sum_plane(b):
        l, _, chunk, _ = BATCHES[b]

        def add(i, total):
            return total + precv[b, i, pl.ds(0, chunk)].astype(F32)

        plane_all(b).wait_recv()
        rows = part(b, plane_me)
        total = lax.fori_loop(0, 15, add, s[l, core, rows] + crecv[l, rows])
        zsend[b, : chunk // 16] = total.reshape(chunk // 16, 16, 128).astype(BF16)

        def send(o):
            @pl.when(jnp.logical_not(mine(b, o)))
            def _():
                z_copy(b, o).start()

        each(0, chunk // 16, send)

    def sum_z(b):
        @pl.when(owns(b))
        def _():
            o = z_hi

            def add(i, total):
                return total + zrecv[b, i].astype(F32)

            z_all(b).wait_recv()

            total = lax.fori_loop(0, 15, add, zsend[b, o].astype(F32))
            zfin[b, o] = (total * (1.0 / 512.0)).astype(BF16)
            each(0, 15, lambda i: z_back(b, i, o).start())

    def spread_plane(b):
        l, _, chunk, _ = BATCHES[b]

        def arrive(o):
            @pl.when(jnp.logical_not(mine(b, o)))
            def _():
                z_back(b, 0, o).wait_recv()

        each(0, chunk // 16, arrive)
        ag[l, core, part(b, plane_me)] = zfin[b, : chunk // 16].reshape(chunk, 128)
        each(0, 15, lambda i: plane_back(b, i).start())
        core_back(b, plane_me).start()

    def out_copy(b, h, n):
        l, base, chunk, _ = BATCHES[b]
        rows = pl.ds(base, min(16 * chunk, HALF - base))
        kernels = pl.ds(base // 64, rows.size // 64)
        return pltpu.make_async_copy(
            ag.reshape(2, 2, 28, 64, 128).at[l, h, kernels], wg.at[l, kernels, h], osem.at[b, n]
        )

    def forward(b):
        def pass_on(t):
            i = 14 - t
            plane_back(b, i).wait_recv()
            core_back(b, plane_from(i)).start()

        each(0, 15, pass_on)
        out_copy(b, core, 0).start()

    def finish(b):
        back_all(b, 16, cas.at[b], car.at[b]).wait_recv()
        out_copy(b, other, 1).start()

    on = maskv[...] > 0
    g1 = jnp.where(on & (pre[1].astype(F32) > 0), cot[...].astype(F32), 0.0)
    x0 = jnp.where(on, feat[...].astype(F32), 0.0)
    stage_corners(0, g1, x0)
    stage_faces(0, g1)
    pl.semaphore_wait(barrier, 8 + 1 + 2 + 15)
    for group in (0, 1):
        for copy in side_copies(group):
            copy.start()
    stage_faces(1, x0)
    for copy in side_copies(2):
        copy.start()
    relay(0)
    place(0, 0, 0, g1.reshape(64, 8, 128))
    place(1, 0, 0, x0.reshape(64, 8, 128))
    x1 = jnp.where(on, jnp.maximum(pre[0].astype(F32), 0.0), 0.0)
    rowsT[0] = x1.T.astype(BF16)
    for f in (0, 1):
        pg[f, :, 27 * 128 :] = jnp.zeros((512, 128), BF16)

    for group in (0, 1):
        for copy in side_copies(group):
            copy.wait_recv()
    rims(0, 0, 0, 0)
    patches(0, -1)
    kernel_grads(1, 0, 8)
    core_copy(0).start()
    kernel_grads(1, 8, 14)
    core_copy(1).start()
    relayed(0)
    relay(1)
    for copy in w_copies:
        copy.wait()
    d1 = input_grads(1)
    g0 = jnp.where((maskv[...] > 0) & (pre[0].astype(F32) > 0), d1, 0.0).astype(BF16).astype(F32)
    stage_corners(1, g0, g0)
    stage_faces(2, g0)
    for group in (3, 4):
        for copy in side_copies(group):
            copy.start()
    rowsT[1] = g0.T.astype(BF16)
    for copy in side_copies(2):
        copy.wait_recv()
    rims(1, 0, 8, 1)
    patches(1, 1)
    sum_halves(0)
    sum_halves(1)
    relayed(1)
    relay(2)
    kernel_grads(0, 0, 8)
    core_copy(2).start()
    kernel_grads(0, 8, 14)
    core_copy(3).start()
    sum_halves(2)
    sum_halves(3)
    relayed(2)
    sum_plane(0)
    sum_plane(1)
    for group in (3, 4):
        for copy in side_copies(group):
            copy.wait_recv()
    place(0, 0, 0, g0.reshape(64, 8, 128))
    rims(0, 1, 0, 2)
    patches(0, -1)
    d0 = input_grads(0)
    gin[...] = jnp.where(maskv[...] > 0, d0, 0.0).astype(BF16)

    sum_plane(2)
    sum_plane(3)
    for group in range(5):
        for copy in side_copies(group):
            copy.wait_send()
    for b in range(4):
        core_copy(b).wait_send()
        plane_all(b).wait_send()
    for b in range(4):
        sum_z(b)
    for b in range(4):

        def sent_z(o):
            @pl.when(jnp.logical_not(mine(b, o)))
            def _():
                z_copy(b, o).wait_send()

        each(0, BATCHES[b][2] // 16, sent_z)
    for b in range(4):
        spread_plane(b)
    for b in range(4):

        @pl.when(owns(b))
        def _():
            z_all(b).wait_send()

    forward(0)
    forward(1)
    finish(0)
    forward(2)
    finish(1)
    forward(3)
    finish(2)
    finish(3)

    for b in range(4):
        back_all(b, 15, pas.at[b], car.at[b]).wait_send()
        back_all(b, 16, cas.at[b], car.at[b]).wait_send()
        out_copy(b, core, 0).wait()
        out_copy(b, other, 1).wait()


def on_device(features, pre_acts, cotangent, weights, voxel_mask, neighbours):
    vmem = pl.BlockSpec(memory_space=pltpu.VMEM)
    anywhere = pl.BlockSpec(memory_space=pl.ANY)
    dma = pltpu.SemaphoreType.DMA
    gin, wg = pl.pallas_call(
        kernel,
        out_shape=(
            jax.ShapeDtypeStruct((512, 128), BF16),
            jax.ShapeDtypeStruct((2, 27, 2, 64, 128), BF16),
        ),
        in_specs=[anywhere] * 6,
        out_specs=(vmem, anywhere),
        scratch_shapes=[
            pltpu.VMEM((512, 128), BF16),
            pltpu.VMEM((2, 512, 128), BF16),
            pltpu.VMEM((512, 128), BF16),
            pltpu.VMEM((1, 512), jnp.int32),
            pltpu.SMEM((1, 27), jnp.int32),
            pltpu.VMEM((2, 27, 128, 128), BF16),
            pltpu.VMEM((512, 128), F32),
            pltpu.VMEM((2, 3, 10, 10, 8, 128), F32),
            pltpu.VMEM((2, 512, 28 * 128), BF16),
            pltpu.VMEM((2, 128, 512), BF16),
            pltpu.VMEM((3, 4, 64, 128), BF16),
            pltpu.VMEM((2, 4, 16, 128), BF16),
            pltpu.VMEM((3, 4, 64, 128), BF16),
            pltpu.VMEM((2, 4, 16, 128), BF16),
            pltpu.VMEM((2, 2, 28 * 64, 128), F32),
            pltpu.VMEM((2, 28 * 64, 128), F32),
            pltpu.VMEM((2, 28 * 64, 128), BF16),
            pltpu.VMEM((4, 15, 64, 128), BF16),
            pltpu.VMEM((4, 4, 16, 128), BF16),
            pltpu.VMEM((4, 15, 16, 128), BF16),
            pltpu.VMEM((4, 4, 16, 128), BF16),
            pltpu.VMEM((2, 2, 28 * 64, 128), BF16),
            dma((5,)), dma((2,)), dma((4, 2)), dma((5, 4)), dma((5, 4)), dma((4,)), dma((4,)),
            dma((4,)), dma((4,)), dma((4, 4)), dma((4,)), dma((4,)), dma((4, 4)),
            dma((4,)), dma((4, 15)), dma((4,)), dma((4,)), pltpu.SemaphoreType.REGULAR((3,)),
        ],
        compiler_params=pltpu.CompilerParams(
            collective_id=0, has_side_effects=True, vmem_limit_bytes=40 * 1024 * 1024
        ),
        cost_estimate=pl.CostEstimate(flops=2_000_000_000, bytes_accessed=5_000_000, transcendentals=0),
    )(
        *(
            pltpu.with_memory_space_constraint(v, pltpu.HBM)
            for v in (
                features.reshape(512, 128),
                pre_acts.reshape(2, 512, 128),
                cotangent.reshape(512, 128),
                voxel_mask.reshape(1, 512),
                neighbours.reshape(1, 27),
                weights,
            )
        )
    )
    return gin.reshape(1, 1, 1, 8, 8, 8, 128), wg.reshape(2, 27, 128, 128)


def solution(mesh):
    in_specs = (
        P("gx", "gy", None, None, None, None, None),
        P(None, "gx", "gy", None, None, None, None, None),
        P("gx", "gy", None, None, None, None, None),
        P(),
        P("gx", "gy", None, None),
        P("gx", "gy", None, None),
    )
    out_specs = (P("gx", "gy", None, None, None, None, None), P())
    return jax.shard_map(
        on_device, mesh=mesh, in_specs=in_specs, out_specs=out_specs, check_vma=False
    )
```

```python
import jax
import jax.numpy as jnp
from jax import lax
from jax.experimental import pallas as pl
from jax.experimental.pallas import tpu as pltpu
from jax.sharding import PartitionSpec as P

F32 = jnp.float32
BF16 = jnp.bfloat16
MESH = pl.DeviceIdType.MESH
SIDES = [(a, b) for a in (-1, 0, 1) for b in (-1, 0, 1) if (a, b) != (0, 0)]
BATCHES = ((1, 0, 64, 0), (1, 1024, 48, 2), (0, 0, 64, 1), (0, 1024, 48, 3))
HALF = 27 * 64


def kernel(
    feat_any, pre_any, cot_any, mask_any, nbr_any, w_any, gin, wg,
    feat, pre, cot, mask, nbr, wv, maskv, pad, pg, rowsT, gface, gcorner, rface, rcorner,
    s, crecv, psend, precv, zsend, zrecv, zfin, ag,
    isem, wsem, osem, hss, hrs, css, crs, pss, prs, zss, zrs, zas, zar, pas, par, cas, car, relays,
):
    gx, gy = lax.axis_index("gx"), lax.axis_index("gy")
    z_hi, x = gx // 4, gx % 4
    y, z_lo, core = gy // 8, (gy // 2) % 4, gy % 2
    other = 1 - core
    plane_me = x * 4 + y
    z_me = z_hi * 4 + z_lo

    def plane_device(i, j):
        return {"gx": z_hi * 4 + i, "gy": j * 8 + z_lo * 2 + core}

    def z_device(i):
        return {"gx": (i // 4) * 4 + x, "gy": y * 8 + (i % 4) * 2 + core}

    core_device = {"gx": gx, "gy": gy + 1 - 2 * core}

    def side_device(a, b):
        return {"gx": (gx + a + 16) % 16, "gy": (gy + b + 32) % 32}

    xs, ys = [(x + d) % 4 for d in range(4)], [(y + d) % 4 for d in range(4)]

    def plane_shift(i):
        v = i + i // 10
        return (2 + v // 4) % 4, (2 + v % 4) % 4

    def plane_to(i):
        dx, dy = plane_shift(i)
        return xs[dx] * 4 + ys[dy]

    def plane_from(i):
        dx, dy = plane_shift(i)
        return xs[-dx] * 4 + ys[-dy]

    def z_far(i):
        return 8 + (i // 2) - (i % 2) * (2 * (i // 2) + 1)

    inputs = [
        pltpu.make_async_copy(src, dst, isem.at[n])
        for n, (src, dst) in enumerate(
            ((mask_any, mask), (nbr_any, nbr), (cot_any, cot), (pre_any, pre), (feat_any, feat))
        )
    ]
    for copy in inputs:
        copy.start()

    barrier = pltpu.get_barrier_semaphore()

    def greet(sem, device):
        pl.semaphore_signal(sem, inc=1, device_id=device, device_id_type=MESH)

    def relay(step):
        for shift in (2**step, 16 - 2**step):
            greet(relays.at[step], z_device((z_me + shift) % 16))

    def relayed(step):
        pl.semaphore_wait(relays.at[step], 2)

    for a, b in SIDES:
        greet(barrier, side_device(a, b))
    greet(barrier, core_device)
    for shift in (1, 15):
        greet(barrier, z_device((z_me + shift) % 16))

    for i in range(15):
        dx, dy = plane_shift(i)
        greet(barrier, plane_device(xs[dx], ys[dy]))
    w_copies = [pltpu.make_async_copy(w_any.at[l], wv.at[l], wsem.at[l]) for l in (1, 0)]
    for copy in w_copies:
        copy.start()

    for copy in inputs:
        copy.wait()
    rows = lax.broadcasted_iota(jnp.int32, (128, 128), 0)
    cols = lax.broadcasted_iota(jnp.int32, (128, 128), 1)
    ones = jnp.ones((128, 128), BF16)
    for r in range(4):
        line = (mask[:, r * 128 : (r + 1) * 128] > 0).astype(F32)
        spread = jnp.where(rows == cols, jnp.broadcast_to(line, (128, 128)), 0.0).astype(BF16)
        maskv[r * 128 : (r + 1) * 128] = jnp.dot(spread, ones, preferred_element_type=F32)

    def flag(a, b, c):
        return jnp.where(nbr[0, (a + 1) * 9 + (b + 1) * 3 + c + 1] >= 0, 1.0, 0.0)

    level = lax.broadcasted_iota(jnp.int32, (1, 8, 128), 1)

    def place(f, a, b, tile):
        low, mid, high = flag(a, b, -1), flag(a, b, 0), flag(a, b, 1)
        nx, ny = (1 if a else 8), (1 if b else 8)
        x0, y0 = {-1: 0, 0: 1, 1: 9}[a], {-1: 0, 0: 1, 1: 9}[b]
        shape = (nx, ny, 8, 128)
        below = pltpu.roll(tile, 1, 1) * jnp.where(level == 0, low, mid)
        above = pltpu.roll(tile, 7, 1) * jnp.where(level == 7, high, mid)
        pad[f, 0, x0 : x0 + nx, y0 : y0 + ny] = below.reshape(shape)
        pad[f, 1, x0 : x0 + nx, y0 : y0 + ny] = (tile * mid).reshape(shape)
        pad[f, 2, x0 : x0 + nx, y0 : y0 + ny] = above.reshape(shape)

    def side_copies(group):
        copies = []
        for a, b in SIDES:
            if (group in (0, 3)) != bool(a and b):
                continue
            if a and b:
                i, j = (a + 1) + (b + 1) // 2, (1 - a) + (1 - b) // 2
                src, dst = gcorner.at[group // 3, i], rcorner.at[group // 3, j]
            else:
                i = (a + 1) // 2 if a else 2 + (b + 1) // 2
                j = (1 - a) // 2 if a else 2 + (1 - b) // 2
                face = {1: 0, 2: 1, 4: 2}[group]
                src, dst = gface.at[face, i], rface.at[face, j]
            copies.append(
                pltpu.make_async_remote_copy(
                    src_ref=src, dst_ref=dst, send_sem=hss.at[group, i], recv_sem=hrs.at[group, j],
                    device_id=side_device(a, b), device_id_type=MESH,
                )
            )
        return copies

    def stage_corners(n, first, second):
        for i in (0, 1):
            for j in (0, 1):
                cells = [v.reshape(8, 8, 8, 128)[7 * i, 7 * j] for v in (first, second)]
                gcorner[n, 2 * i + j] = jnp.concatenate(cells, axis=0).astype(BF16)

    def stage_faces(n, v):
        v4 = v.reshape(8, 8, 8, 128)
        for i in (0, 1):
            gface[n, i] = v4[7 * i].reshape(64, 128).astype(BF16)
            gface[n, 2 + i] = v4[:, 7 * i].reshape(64, 128).astype(BF16)

    def rims(f, corners, row, face):
        for a, b in SIDES:
            if a and b:
                cell = rcorner[corners, (a + 1) + (b + 1) // 2].astype(F32)[row : row + 8]
                place(f, a, b, cell.reshape(1, 8, 128))
            else:
                i = (a + 1) // 2 if a else 2 + (b + 1) // 2
                place(f, a, b, rface[face, i].astype(F32).reshape(8, 8, 128))

    def patches(f, sign):
        for k in range(27):
            a, b, c = (sign * v for v in (k // 9 - 1, (k // 3) % 3 - 1, k % 3 - 1))
            window = pad[f, 1 + c, 1 + a : 9 + a, 1 + b : 9 + b]
            pg[f, :, k * 128 : (k + 1) * 128] = window.reshape(512, 128).astype(BF16)

    def input_grads(l):
        kernels = jnp.concatenate([wv[l, k] for k in range(27)], axis=1)
        return lax.dot_general(
            pg[0, :, : 27 * 128], kernels, (((1,), (1,)), ((), ())), preferred_element_type=F32
        )

    def kernel_grads(l, first, last):
        f = 1 - l
        for m in range(first, last):
            both = jnp.dot(
                rowsT[f], pg[f, :, m * 256 : (m + 1) * 256], preferred_element_type=F32
            )
            for q in (0, 1):
                block = both[:, q * 128 : (q + 1) * 128]
                block = block.T if l == 0 else block
                for h in (0, 1):
                    at = m * 128 + q * 64
                    s[l, h, at : at + 64] = block[h * 64 : (h + 1) * 64]

    def part(b, i):
        _, base, chunk, _ = BATCHES[b]
        return pl.ds(pl.multiple_of(base + i * chunk, 16), chunk)

    def core_copy(b):
        l, base, chunk, _ = BATCHES[b]
        rows = pl.ds(base, 16 * chunk)
        return pltpu.make_async_remote_copy(
            src_ref=s.at[l, other, rows], dst_ref=crecv.at[l, rows],
            send_sem=css.at[b], recv_sem=crs.at[b],
            device_id=core_device, device_id_type=MESH,
        )

    def plane_copy(b, i):
        l, _, chunk, _ = BATCHES[b]
        peer, (dx, dy) = plane_to(i), plane_shift(i)
        return pltpu.make_async_remote_copy(
            src_ref=psend.at[l, part(b, peer)], dst_ref=precv.at[b, i, pl.ds(0, chunk)],
            send_sem=pss.at[b], recv_sem=prs.at[b],
            device_id=plane_device(xs[dx], ys[dy]), device_id_type=MESH,
        )

    def z_copy(b, o):
        owner = BATCHES[b][3] + 4 * o
        return pltpu.make_async_remote_copy(
            src_ref=zsend.at[b, o], dst_ref=zrecv.at[b, (owner + 15 - z_me) % 16],
            send_sem=zss.at[b, o], recv_sem=zrs.at[b],
            device_id=z_device(owner), device_id_type=MESH,
        )

    def bytes_of(ref, send_sem, recv_sem):
        return pltpu.make_async_remote_copy(
            src_ref=ref, dst_ref=ref, send_sem=send_sem, recv_sem=recv_sem,
            device_id=core_device, device_id_type=MESH,
        )

    def plane_all(b):
        return bytes_of(precv.at[b, :, pl.ds(0, BATCHES[b][2])], pss.at[b], prs.at[b])

    def z_all(b):
        return bytes_of(zrecv.at[b], zas.at[b], zrs.at[b])

    def back_all(b, count, send_sem, recv_sem):
        l, base, chunk, _ = BATCHES[b]
        return bytes_of(ag.at[l, core, pl.ds(base, count * chunk)], send_sem, recv_sem)

    def z_back(b, i, o):
        return pltpu.make_async_remote_copy(
            src_ref=zfin.at[b, o], dst_ref=zfin.at[b, o],
            send_sem=zas.at[b], recv_sem=zar.at[b, o],
            device_id=z_device((z_me + z_far(i)) % 16), device_id_type=MESH,
        )

    def plane_back(b, i):
        l = BATCHES[b][0]
        rows = part(b, plane_me)
        dx, dy = plane_shift(i)
        return pltpu.make_async_remote_copy(
            src_ref=ag.at[l, core, rows], dst_ref=ag.at[l, core, rows],
            send_sem=pas.at[b], recv_sem=par.at[b, i],
            device_id=plane_device(xs[dx], ys[dy]), device_id_type=MESH,
        )

    def core_back(b, owner):
        l = BATCHES[b][0]
        rows = part(b, owner)
        return pltpu.make_async_remote_copy(
            src_ref=ag.at[l, core, rows], dst_ref=ag.at[l, core, rows],
            send_sem=cas.at[b], recv_sem=car.at[b],
            device_id=core_device, device_id_type=MESH,
        )

    def each(first, last, act):
        for j in range(first, last):
            act(j)

    def sum_halves(b):
        l = BATCHES[b][0]
        core_copy(b).wait_recv()

        def chunk(i):
            rows = part(b, plane_to(i))
            psend[l, rows] = (s[l, core, rows] + crecv[l, rows]).astype(BF16)
            plane_copy(b, i).start()

        each(0, 15, chunk)

    def mine(b, o):
        return (z_lo == BATCHES[b][3]) & (z_hi == o)

    def owns(b):
        return (z_lo == BATCHES[b][3]) & (z_hi < BATCHES[b][2] // 16)

    def sum_plane(b):
        l, _, chunk, _ = BATCHES[b]

        plane_all(b).wait_recv()
        rows = part(b, plane_me)
        total = s[l, core, rows] + crecv[l, rows]
        for i in range(15):
            total = total + precv[b, i, :chunk].astype(F32)
        zsend[b, : chunk // 16] = total.reshape(chunk // 16, 16, 128).astype(BF16)

        def send(o):
            @pl.when(jnp.logical_not(mine(b, o)))
            def _():
                z_copy(b, o).start()

        each(0, chunk // 16, send)

    def sum_z(b):
        @pl.when(owns(b))
        def _():
            o = z_hi

            z_all(b).wait_recv()
            total = zsend[b, o].astype(F32)
            for i in range(15):
                total = total + zrecv[b, i].astype(F32)
            zfin[b, o] = (total * (1.0 / 512.0)).astype(BF16)
            each(0, 15, lambda i: z_back(b, i, o).start())

    def spread_plane(b):
        l, _, chunk, _ = BATCHES[b]

        def arrive(o):
            @pl.when(jnp.logical_not(mine(b, o)))
            def _():
                z_back(b, 0, o).wait_recv()

        each(0, chunk // 16, arrive)
        ag[l, core, part(b, plane_me)] = zfin[b, : chunk // 16].reshape(chunk, 128)
        each(0, 15, lambda i: plane_back(b, i).start())
        core_back(b, plane_me).start()

    def out_copy(b, h, n):
        l, base, chunk, _ = BATCHES[b]
        rows = pl.ds(base, min(16 * chunk, HALF - base))
        kernels = pl.ds(base // 64, rows.size // 64)
        return pltpu.make_async_copy(
            ag.reshape(2, 2, 28, 64, 128).at[l, h, kernels], wg.at[l, kernels, h], osem.at[b, n]
        )

    def forward(b):
        def pass_on(t):
            i = 14 - t
            plane_back(b, i).wait_recv()
            core_back(b, plane_from(i)).start()

        each(0, 15, pass_on)
        out_copy(b, core, 0).start()

    def finish(b):
        back_all(b, 16, cas.at[b], car.at[b]).wait_recv()
        out_copy(b, other, 1).start()

    on = maskv[...] > 0
    g1 = jnp.where(on & (pre[1].astype(F32) > 0), cot[...].astype(F32), 0.0)
    x0 = jnp.where(on, feat[...].astype(F32), 0.0)
    stage_corners(0, g1, x0)
    stage_faces(0, g1)
    pl.semaphore_wait(barrier, 8 + 1 + 2 + 15)
    for group in (0, 1):
        for copy in side_copies(group):
            copy.start()
    stage_faces(1, x0)
    for copy in side_copies(2):
        copy.start()
    relay(0)
    place(0, 0, 0, g1.reshape(64, 8, 128))
    place(1, 0, 0, x0.reshape(64, 8, 128))
    x1 = jnp.where(on, jnp.maximum(pre[0].astype(F32), 0.0), 0.0)
    rowsT[0] = x1.T.astype(BF16)
    for f in (0, 1):
        pg[f, :, 27 * 128 :] = jnp.zeros((512, 128), BF16)

    for group in (0, 1):
        for copy in side_copies(group):
            copy.wait_recv()
    rims(0, 0, 0, 0)
    patches(0, -1)
    kernel_grads(1, 0, 8)
    core_copy(0).start()
    kernel_grads(1, 8, 14)
    core_copy(1).start()
    relayed(0)
    relay(1)
    for copy in w_copies:
        copy.wait()
    d1 = input_grads(1)
    g0 = jnp.where((maskv[...] > 0) & (pre[0].astype(F32) > 0), d1, 0.0).astype(BF16).astype(F32)
    stage_corners(1, g0, g0)
    stage_faces(2, g0)
    for group in (3, 4):
        for copy in side_copies(group):
            copy.start()
    rowsT[1] = g0.T.astype(BF16)
    for copy in side_copies(2):
        copy.wait_recv()
    rims(1, 0, 8, 1)
    patches(1, 1)
    sum_halves(0)
    sum_halves(1)
    relayed(1)
    relay(2)
    kernel_grads(0, 0, 8)
    core_copy(2).start()
    kernel_grads(0, 8, 14)
    core_copy(3).start()
    sum_halves(2)
    sum_halves(3)
    relayed(2)
    sum_plane(0)
    sum_plane(1)
    for group in (3, 4):
        for copy in side_copies(group):
            copy.wait_recv()
    place(0, 0, 0, g0.reshape(64, 8, 128))
    rims(0, 1, 0, 2)
    patches(0, -1)
    d0 = input_grads(0)
    gin[...] = jnp.where(maskv[...] > 0, d0, 0.0).astype(BF16)

    sum_plane(2)
    sum_plane(3)
    for group in range(5):
        for copy in side_copies(group):
            copy.wait_send()
    for b in range(4):
        core_copy(b).wait_send()
        plane_all(b).wait_send()
    for b in range(4):
        sum_z(b)
    for b in range(4):

        def sent_z(o):
            @pl.when(jnp.logical_not(mine(b, o)))
            def _():
                z_copy(b, o).wait_send()

        each(0, BATCHES[b][2] // 16, sent_z)
    for b in range(4):
        spread_plane(b)
    for b in range(4):

        @pl.when(owns(b))
        def _():
            z_all(b).wait_send()

    forward(0)
    forward(1)
    finish(0)
    forward(2)
    finish(1)
    forward(3)
    finish(2)
    finish(3)

    for b in range(4):
        back_all(b, 15, pas.at[b], car.at[b]).wait_send()
        back_all(b, 16, cas.at[b], car.at[b]).wait_send()
        out_copy(b, core, 0).wait()
        out_copy(b, other, 1).wait()


def on_device(features, pre_acts, cotangent, weights, voxel_mask, neighbours):
    vmem = pl.BlockSpec(memory_space=pltpu.VMEM)
    anywhere = pl.BlockSpec(memory_space=pl.ANY)
    dma = pltpu.SemaphoreType.DMA
    gin, wg = pl.pallas_call(
        kernel,
        out_shape=(
            jax.ShapeDtypeStruct((512, 128), BF16),
            jax.ShapeDtypeStruct((2, 27, 2, 64, 128), BF16),
        ),
        in_specs=[anywhere] * 6,
        out_specs=(vmem, anywhere),
        scratch_shapes=[
            pltpu.VMEM((512, 128), BF16),
            pltpu.VMEM((2, 512, 128), BF16),
            pltpu.VMEM((512, 128), BF16),
            pltpu.VMEM((1, 512), jnp.int32),
            pltpu.SMEM((1, 27), jnp.int32),
            pltpu.VMEM((2, 27, 128, 128), BF16),
            pltpu.VMEM((512, 128), F32),
            pltpu.VMEM((2, 3, 10, 10, 8, 128), F32),
            pltpu.VMEM((2, 512, 28 * 128), BF16),
            pltpu.VMEM((2, 128, 512), BF16),
            pltpu.VMEM((3, 4, 64, 128), BF16),
            pltpu.VMEM((2, 4, 16, 128), BF16),
            pltpu.VMEM((3, 4, 64, 128), BF16),
            pltpu.VMEM((2, 4, 16, 128), BF16),
            pltpu.VMEM((2, 2, 28 * 64, 128), F32),
            pltpu.VMEM((2, 28 * 64, 128), F32),
            pltpu.VMEM((2, 28 * 64, 128), BF16),
            pltpu.VMEM((4, 15, 64, 128), BF16),
            pltpu.VMEM((4, 4, 16, 128), BF16),
            pltpu.VMEM((4, 15, 16, 128), BF16),
            pltpu.VMEM((4, 4, 16, 128), BF16),
            pltpu.VMEM((2, 2, 28 * 64, 128), BF16),
            dma((5,)), dma((2,)), dma((4, 2)), dma((5, 4)), dma((5, 4)), dma((4,)), dma((4,)),
            dma((4,)), dma((4,)), dma((4, 4)), dma((4,)), dma((4,)), dma((4, 4)),
            dma((4,)), dma((4, 15)), dma((4,)), dma((4,)), pltpu.SemaphoreType.REGULAR((3,)),
        ],
        compiler_params=pltpu.CompilerParams(
            collective_id=0, has_side_effects=True, vmem_limit_bytes=40 * 1024 * 1024
        ),
        cost_estimate=pl.CostEstimate(flops=2_000_000_000, bytes_accessed=5_000_000, transcendentals=0),
    )(
        *(
            pltpu.with_memory_space_constraint(v, pltpu.HBM)
            for v in (
                features.reshape(512, 128),
                pre_acts.reshape(2, 512, 128),
                cotangent.reshape(512, 128),
                voxel_mask.reshape(1, 512),
                neighbours.reshape(1, 27),
                weights,
            )
        )
    )
    return gin.reshape(1, 1, 1, 8, 8, 8, 128), wg.reshape(2, 27, 128, 128)


def solution(mesh):
    in_specs = (
        P("gx", "gy", None, None, None, None, None),
        P(None, "gx", "gy", None, None, None, None, None),
        P("gx", "gy", None, None, None, None, None),
        P(),
        P("gx", "gy", None, None),
        P("gx", "gy", None, None),
    )
    out_specs = (P("gx", "gy", None, None, None, None, None), P())
    return jax.shard_map(
        on_device, mesh=mesh, in_specs=in_specs, out_specs=out_specs, check_vma=False
    )
```

```python
import jax
import jax.numpy as jnp
from jax import lax
from jax.experimental import pallas as pl
from jax.experimental.pallas import tpu as pltpu
from jax.sharding import PartitionSpec as P

F32 = jnp.float32
BF16 = jnp.bfloat16
MESH = pl.DeviceIdType.MESH
SIDES = [(a, b) for a in (-1, 0, 1) for b in (-1, 0, 1) if (a, b) != (0, 0)]
BATCHES = ((1, 0, 64, 0), (1, 1024, 48, 2), (0, 0, 64, 1), (0, 1024, 48, 3))
HALF = 27 * 64
SHIFTS = (
    (2, 2), (3, 1), (0, 2), (1, 3), (2, 0), (3, 2), (2, 1), (1, 2),
    (0, 1), (3, 3), (2, 3), (1, 0), (0, 3), (1, 1), (3, 0),
)


def kernel(
    feat_any, pre_any, cot_any, mask_any, nbr_any, w_any, gin, wg,
    feat, pre, cot, mask, nbr, wv, maskv, pad, pg, rowsT, gface, gcorner, rface, rcorner,
    s, sent, crecv, psend, precv, zsend, zrecv, zfin, ag,
    isem, wsem, osem, hss, hrs, css, crs, pss, prs, zss, zrs, zas, zar, pas, par, cas, car, relays,
):
    gx, gy = lax.axis_index("gx"), lax.axis_index("gy")
    z_hi, x = gx // 4, gx % 4
    y, z_lo, core = gy // 8, (gy // 2) % 4, gy % 2
    other = 1 - core
    plane_me = x * 4 + y
    z_me = z_hi * 4 + z_lo

    def plane_device(i, j):
        return {"gx": z_hi * 4 + i, "gy": j * 8 + z_lo * 2 + core}

    def z_device(i):
        return {"gx": (i // 4) * 4 + x, "gy": y * 8 + (i % 4) * 2 + core}

    core_device = {"gx": gx, "gy": gy + 1 - 2 * core}

    def side_device(a, b):
        return {"gx": (gx + a + 16) % 16, "gy": (gy + b + 32) % 32}

    xs, ys = [(x + d) % 4 for d in range(4)], [(y + d) % 4 for d in range(4)]

    def plane_shift(i):
        return SHIFTS[i]

    def plane_to(i):
        dx, dy = plane_shift(i)
        return xs[dx] * 4 + ys[dy]

    def plane_from(i):
        dx, dy = plane_shift(i)
        return xs[-dx] * 4 + ys[-dy]

    def z_far(i):
        return 8 + (i // 2) - (i % 2) * (2 * (i // 2) + 1)

    inputs = [
        pltpu.make_async_copy(src, dst, isem.at[n])
        for n, (src, dst) in enumerate(
            ((mask_any, mask), (nbr_any, nbr), (cot_any, cot), (pre_any, pre), (feat_any, feat))
        )
    ]
    for copy in inputs:
        copy.start()

    barrier = pltpu.get_barrier_semaphore()

    def greet(sem, device):
        pl.semaphore_signal(sem, inc=1, device_id=device, device_id_type=MESH)

    def relay(step):
        for shift in (2**step, 16 - 2**step):
            greet(relays.at[step], z_device((z_me + shift) % 16))

    def relayed(step):
        pl.semaphore_wait(relays.at[step], 2)

    for a, b in SIDES:
        greet(barrier, side_device(a, b))
    greet(barrier, core_device)
    for shift in (1, 15):
        greet(barrier, z_device((z_me + shift) % 16))

    for i in range(15):
        dx, dy = plane_shift(i)
        greet(barrier, plane_device(xs[dx], ys[dy]))
    w_copies = [pltpu.make_async_copy(w_any.at[l], wv.at[l], wsem.at[l]) for l in (1, 0)]
    for copy in w_copies:
        copy.start()

    for copy in inputs:
        copy.wait()
    rows = lax.broadcasted_iota(jnp.int32, (128, 128), 0)
    cols = lax.broadcasted_iota(jnp.int32, (128, 128), 1)
    ones = jnp.ones((128, 128), BF16)
    for r in range(4):
        line = (mask[:, r * 128 : (r + 1) * 128] > 0).astype(F32)
        spread = jnp.where(rows == cols, jnp.broadcast_to(line, (128, 128)), 0.0).astype(BF16)
        maskv[r * 128 : (r + 1) * 128] = jnp.dot(spread, ones, preferred_element_type=F32)

    def flag(a, b, c):
        return jnp.where(nbr[0, (a + 1) * 9 + (b + 1) * 3 + c + 1] >= 0, 1.0, 0.0)

    level = lax.broadcasted_iota(jnp.int32, (1, 8, 128), 1)

    def place(f, a, b, tile):
        low, mid, high = flag(a, b, -1), flag(a, b, 0), flag(a, b, 1)
        nx, ny = (1 if a else 8), (1 if b else 8)
        x0, y0 = {-1: 0, 0: 1, 1: 9}[a], {-1: 0, 0: 1, 1: 9}[b]
        shape = (nx, ny, 8, 128)
        below = pltpu.roll(tile, 1, 1) * jnp.where(level == 0, low, mid)
        above = pltpu.roll(tile, 7, 1) * jnp.where(level == 7, high, mid)
        pad[f, 0, x0 : x0 + nx, y0 : y0 + ny] = below.reshape(shape)
        pad[f, 1, x0 : x0 + nx, y0 : y0 + ny] = (tile * mid).reshape(shape)
        pad[f, 2, x0 : x0 + nx, y0 : y0 + ny] = above.reshape(shape)

    def side_copies(group):
        copies = []
        for a, b in SIDES:
            if (group in (0, 3)) != bool(a and b):
                continue
            if a and b:
                i, j = (a + 1) + (b + 1) // 2, (1 - a) + (1 - b) // 2
                src, dst = gcorner.at[group // 3, i], rcorner.at[group // 3, j]
            else:
                i = (a + 1) // 2 if a else 2 + (b + 1) // 2
                j = (1 - a) // 2 if a else 2 + (1 - b) // 2
                face = {1: 0, 2: 1, 4: 2}[group]
                src, dst = gface.at[face, i], rface.at[face, j]
            copies.append(
                pltpu.make_async_remote_copy(
                    src_ref=src, dst_ref=dst, send_sem=hss.at[group, i], recv_sem=hrs.at[group, j],
                    device_id=side_device(a, b), device_id_type=MESH,
                )
            )
        return copies

    def stage_corners(n, first, second):
        for i in (0, 1):
            for j in (0, 1):
                cells = [v.reshape(8, 8, 8, 128)[7 * i, 7 * j] for v in (first, second)]
                gcorner[n, 2 * i + j] = jnp.concatenate(cells, axis=0).astype(BF16)

    def stage_faces(n, v):
        v4 = v.reshape(8, 8, 8, 128)
        for i in (0, 1):
            gface[n, i] = v4[7 * i].reshape(64, 128).astype(BF16)
            gface[n, 2 + i] = v4[:, 7 * i].reshape(64, 128).astype(BF16)

    def rims(f, corners, row, face):
        for a, b in SIDES:
            if a and b:
                cell = rcorner[corners, (a + 1) + (b + 1) // 2].astype(F32)[row : row + 8]
                place(f, a, b, cell.reshape(1, 8, 128))
            else:
                i = (a + 1) // 2 if a else 2 + (b + 1) // 2
                place(f, a, b, rface[face, i].astype(F32).reshape(8, 8, 128))

    def patches(f, sign):
        for k in range(27):
            a, b, c = (sign * v for v in (k // 9 - 1, (k // 3) % 3 - 1, k % 3 - 1))
            window = pad[f, 1 + c, 1 + a : 9 + a, 1 + b : 9 + b]
            pg[f, :, k * 128 : (k + 1) * 128] = window.reshape(512, 128).astype(BF16)

    def input_grads(l):
        kernels = jnp.concatenate([wv[l, k] for k in range(27)], axis=1)
        return lax.dot_general(
            pg[0, :, : 27 * 128], kernels, (((1,), (1,)), ((), ())), preferred_element_type=F32
        )

    def kernel_grads(l, first, last):
        f = 1 - l
        for m in range(first, last):
            both = jnp.dot(
                rowsT[f], pg[f, :, m * 256 : (m + 1) * 256], preferred_element_type=F32
            )
            for q in (0, 1):
                block = both[:, q * 128 : (q + 1) * 128]
                block = block.T if l == 0 else block
                for h in (0, 1):
                    at = m * 128 + q * 64
                    s[l, h, at : at + 64] = block[h * 64 : (h + 1) * 64]
                    sent[l, h, at : at + 64] = block[h * 64 : (h + 1) * 64].astype(BF16)

    def part(b, i):
        _, base, chunk, _ = BATCHES[b]
        return pl.ds(pl.multiple_of(base + i * chunk, 16), chunk)

    def core_copy(b):
        l, base, chunk, _ = BATCHES[b]
        rows = pl.ds(base, 16 * chunk)
        return pltpu.make_async_remote_copy(
            src_ref=sent.at[l, other, rows], dst_ref=crecv.at[l, rows],
            send_sem=css.at[b], recv_sem=crs.at[b],
            device_id=core_device, device_id_type=MESH,
        )

    def plane_copy(b, i):
        l, _, chunk, _ = BATCHES[b]
        peer, (dx, dy) = plane_to(i), plane_shift(i)
        return pltpu.make_async_remote_copy(
            src_ref=psend.at[l, part(b, peer)], dst_ref=precv.at[b, i, pl.ds(0, chunk)],
            send_sem=pss.at[b], recv_sem=prs.at[b],
            device_id=plane_device(xs[dx], ys[dy]), device_id_type=MESH,
        )

    def z_copy(b, o):
        owner = BATCHES[b][3] + 4 * o
        return pltpu.make_async_remote_copy(
            src_ref=zsend.at[b, o], dst_ref=zrecv.at[b, (owner + 15 - z_me) % 16],
            send_sem=zss.at[b, o], recv_sem=zrs.at[b],
            device_id=z_device(owner), device_id_type=MESH,
        )

    def bytes_of(ref, send_sem, recv_sem):
        return pltpu.make_async_remote_copy(
            src_ref=ref, dst_ref=ref, send_sem=send_sem, recv_sem=recv_sem,
            device_id=core_device, device_id_type=MESH,
        )

    def plane_all(b):
        return bytes_of(precv.at[b, :, pl.ds(0, BATCHES[b][2])], pss.at[b], prs.at[b])

    def z_all(b):
        return bytes_of(zrecv.at[b], zas.at[b], zrs.at[b])

    def back_all(b, count, send_sem, recv_sem):
        l, base, chunk, _ = BATCHES[b]
        return bytes_of(ag.at[l, core, pl.ds(base, count * chunk)], send_sem, recv_sem)

    def z_back(b, i, o):
        return pltpu.make_async_remote_copy(
            src_ref=zfin.at[b, o], dst_ref=zfin.at[b, o],
            send_sem=zas.at[b], recv_sem=zar.at[b, o],
            device_id=z_device((z_me + z_far(i)) % 16), device_id_type=MESH,
        )

    def plane_back(b, i):
        l = BATCHES[b][0]
        rows = part(b, plane_me)
        dx, dy = plane_shift(i)
        return pltpu.make_async_remote_copy(
            src_ref=ag.at[l, core, rows], dst_ref=ag.at[l, core, rows],
            send_sem=pas.at[b], recv_sem=par.at[b, i],
            device_id=plane_device(xs[dx], ys[dy]), device_id_type=MESH,
        )

    def core_back(b, owner):
        l = BATCHES[b][0]
        rows = part(b, owner)
        return pltpu.make_async_remote_copy(
            src_ref=ag.at[l, core, rows], dst_ref=ag.at[l, core, rows],
            send_sem=cas.at[b], recv_sem=car.at[b],
            device_id=core_device, device_id_type=MESH,
        )

    def each(first, last, act):
        for j in range(first, last):
            act(j)

    def sum_halves(b):
        l = BATCHES[b][0]
        core_copy(b).wait_recv()

        def chunk(i):
            rows = part(b, plane_to(i))
            psend[l, rows] = (s[l, core, rows] + crecv[l, rows].astype(F32)).astype(BF16)
            plane_copy(b, i).start()

        each(0, 15, chunk)

    def mine(b, o):
        return (z_lo == BATCHES[b][3]) & (z_hi == o)

    def owns(b):
        return (z_lo == BATCHES[b][3]) & (z_hi < BATCHES[b][2] // 16)

    def sum_plane(b):
        l, _, chunk, _ = BATCHES[b]

        plane_all(b).wait_recv()
        rows = part(b, plane_me)
        total = s[l, core, rows] + crecv[l, rows].astype(F32)
        for i in range(15):
            total = total + precv[b, i, :chunk].astype(F32)
        zsend[b, : chunk // 16] = total.reshape(chunk // 16, 16, 128).astype(BF16)

        def send(o):
            @pl.when(jnp.logical_not(mine(b, o)))
            def _():
                z_copy(b, o).start()

        each(0, chunk // 16, send)

    def sum_z(b):
        @pl.when(owns(b))
        def _():
            o = z_hi

            z_all(b).wait_recv()
            total = zsend[b, o].astype(F32)
            for i in range(15):
                total = total + zrecv[b, i].astype(F32)
            zfin[b, o] = (total * (1.0 / 512.0)).astype(BF16)
            each(0, 15, lambda i: z_back(b, i, o).start())

    def spread_plane(b):
        l, _, chunk, _ = BATCHES[b]

        def arrive(o):
            @pl.when(jnp.logical_not(mine(b, o)))
            def _():
                z_back(b, 0, o).wait_recv()

        each(0, chunk // 16, arrive)
        ag[l, core, part(b, plane_me)] = zfin[b, : chunk // 16].reshape(chunk, 128)
        each(0, 15, lambda i: plane_back(b, i).start())
        core_back(b, plane_me).start()

    def out_copy(b, h, n):
        l, base, chunk, _ = BATCHES[b]
        rows = pl.ds(base, min(16 * chunk, HALF - base))
        kernels = pl.ds(base // 64, rows.size // 64)
        return pltpu.make_async_copy(
            ag.reshape(2, 2, 28, 64, 128).at[l, h, kernels], wg.at[l, kernels, h], osem.at[b, n]
        )

    def forward(b):
        def pass_on(t):
            i = 14 - t
            plane_back(b, i).wait_recv()
            core_back(b, plane_from(i)).start()

        each(0, 15, pass_on)
        out_copy(b, core, 0).start()

    def finish(b):
        back_all(b, 16, cas.at[b], car.at[b]).wait_recv()
        out_copy(b, other, 1).start()

    on = maskv[...] > 0
    g1 = jnp.where(on & (pre[1].astype(F32) > 0), cot[...].astype(F32), 0.0)
    x0 = jnp.where(on, feat[...].astype(F32), 0.0)
    stage_corners(0, g1, x0)
    stage_faces(0, g1)
    pl.semaphore_wait(barrier, 8 + 1 + 2 + 15)
    for group in (0, 1):
        for copy in side_copies(group):
            copy.start()
    stage_faces(1, x0)
    for copy in side_copies(2):
        copy.start()
    relay(0)
    place(0, 0, 0, g1.reshape(64, 8, 128))
    place(1, 0, 0, x0.reshape(64, 8, 128))
    x1 = jnp.where(on, jnp.maximum(pre[0].astype(F32), 0.0), 0.0)
    rowsT[0] = x1.T.astype(BF16)
    for f in (0, 1):
        pg[f, :, 27 * 128 :] = jnp.zeros((512, 128), BF16)

    for group in (0, 1):
        for copy in side_copies(group):
            copy.wait_recv()
    rims(0, 0, 0, 0)
    patches(0, -1)
    kernel_grads(1, 0, 8)
    core_copy(0).start()
    kernel_grads(1, 8, 14)
    core_copy(1).start()
    relayed(0)
    relay(1)
    for copy in w_copies:
        copy.wait()
    d1 = input_grads(1)
    g0 = jnp.where((maskv[...] > 0) & (pre[0].astype(F32) > 0), d1, 0.0).astype(BF16).astype(F32)
    stage_corners(1, g0, g0)
    stage_faces(2, g0)
    for group in (3, 4):
        for copy in side_copies(group):
            copy.start()
    rowsT[1] = g0.T.astype(BF16)
    for copy in side_copies(2):
        copy.wait_recv()
    rims(1, 0, 8, 1)
    patches(1, 1)
    sum_halves(0)
    sum_halves(1)
    relayed(1)
    relay(2)
    kernel_grads(0, 0, 8)
    core_copy(2).start()
    kernel_grads(0, 8, 14)
    core_copy(3).start()
    sum_halves(2)
    sum_halves(3)
    relayed(2)
    sum_plane(0)
    sum_plane(1)
    for group in (3, 4):
        for copy in side_copies(group):
            copy.wait_recv()
    place(0, 0, 0, g0.reshape(64, 8, 128))
    rims(0, 1, 0, 2)
    patches(0, -1)
    d0 = input_grads(0)
    gin[...] = jnp.where(maskv[...] > 0, d0, 0.0).astype(BF16)

    sum_plane(2)
    sum_plane(3)
    for group in range(5):
        for copy in side_copies(group):
            copy.wait_send()
    for b in range(4):
        core_copy(b).wait_send()
        plane_all(b).wait_send()
    for b in range(4):
        sum_z(b)
    for b in range(4):

        def sent_z(o):
            @pl.when(jnp.logical_not(mine(b, o)))
            def _():
                z_copy(b, o).wait_send()

        each(0, BATCHES[b][2] // 16, sent_z)
    for b in range(4):
        spread_plane(b)
    for b in range(4):

        @pl.when(owns(b))
        def _():
            z_all(b).wait_send()

    forward(0)
    forward(1)
    finish(0)
    forward(2)
    finish(1)
    forward(3)
    finish(2)
    finish(3)

    for b in range(4):
        back_all(b, 15, pas.at[b], car.at[b]).wait_send()
        back_all(b, 16, cas.at[b], car.at[b]).wait_send()
        out_copy(b, core, 0).wait()
        out_copy(b, other, 1).wait()


def on_device(features, pre_acts, cotangent, weights, voxel_mask, neighbours):
    vmem = pl.BlockSpec(memory_space=pltpu.VMEM)
    anywhere = pl.BlockSpec(memory_space=pl.ANY)
    dma = pltpu.SemaphoreType.DMA
    gin, wg = pl.pallas_call(
        kernel,
        out_shape=(
            jax.ShapeDtypeStruct((512, 128), BF16),
            jax.ShapeDtypeStruct((2, 27, 2, 64, 128), BF16),
        ),
        in_specs=[anywhere] * 6,
        out_specs=(vmem, anywhere),
        scratch_shapes=[
            pltpu.VMEM((512, 128), BF16),
            pltpu.VMEM((2, 512, 128), BF16),
            pltpu.VMEM((512, 128), BF16),
            pltpu.VMEM((1, 512), jnp.int32),
            pltpu.SMEM((1, 27), jnp.int32),
            pltpu.VMEM((2, 27, 128, 128), BF16),
            pltpu.VMEM((512, 128), F32),
            pltpu.VMEM((2, 3, 10, 10, 8, 128), F32),
            pltpu.VMEM((2, 512, 28 * 128), BF16),
            pltpu.VMEM((2, 128, 512), BF16),
            pltpu.VMEM((3, 4, 64, 128), BF16),
            pltpu.VMEM((2, 4, 16, 128), BF16),
            pltpu.VMEM((3, 4, 64, 128), BF16),
            pltpu.VMEM((2, 4, 16, 128), BF16),
            pltpu.VMEM((2, 2, 28 * 64, 128), F32),
            pltpu.VMEM((2, 2, 28 * 64, 128), BF16),
            pltpu.VMEM((2, 28 * 64, 128), BF16),
            pltpu.VMEM((2, 28 * 64, 128), BF16),
            pltpu.VMEM((4, 15, 64, 128), BF16),
            pltpu.VMEM((4, 4, 16, 128), BF16),
            pltpu.VMEM((4, 15, 16, 128), BF16),
            pltpu.VMEM((4, 4, 16, 128), BF16),
            pltpu.VMEM((2, 2, 28 * 64, 128), BF16),
            dma((5,)), dma((2,)), dma((4, 2)), dma((5, 4)), dma((5, 4)), dma((4,)), dma((4,)),
            dma((4,)), dma((4,)), dma((4, 4)), dma((4,)), dma((4,)), dma((4, 4)),
            dma((4,)), dma((4, 15)), dma((4,)), dma((4,)), pltpu.SemaphoreType.REGULAR((3,)),
        ],
        compiler_params=pltpu.CompilerParams(
            collective_id=0, has_side_effects=True, vmem_limit_bytes=40 * 1024 * 1024
        ),
        cost_estimate=pl.CostEstimate(flops=2_000_000_000, bytes_accessed=5_000_000, transcendentals=0),
    )(
        *(
            pltpu.with_memory_space_constraint(v, pltpu.HBM)
            for v in (
                features.reshape(512, 128),
                pre_acts.reshape(2, 512, 128),
                cotangent.reshape(512, 128),
                voxel_mask.reshape(1, 512),
                neighbours.reshape(1, 27),
                weights,
            )
        )
    )
    return gin.reshape(1, 1, 1, 8, 8, 8, 128), wg.reshape(2, 27, 128, 128)


def solution(mesh):
    in_specs = (
        P("gx", "gy", None, None, None, None, None),
        P(None, "gx", "gy", None, None, None, None, None),
        P("gx", "gy", None, None, None, None, None),
        P(),
        P("gx", "gy", None, None),
        P("gx", "gy", None, None),
    )
    out_specs = (P("gx", "gy", None, None, None, None, None), P())
    return jax.shard_map(
        on_device, mesh=mesh, in_specs=in_specs, out_specs=out_specs, check_vma=False
    )
```
